32 devices in a mesh: seq: 8 (over y, x, core), tp: 4 (over z).
Axes of the slice: x: 2, y: 2, z: 4, core: 2. Of those that a mesh axis runs over, the one named last changes fastest.
Arguments:
- tokens: bfloat16 [8192, 2048], P('seq'), may hold values from -6 to 6
- doc_start: int32 [8192], P('seq'), may hold values from 0 to 1, as said below
- norm_first: bfloat16 [2048], replicated, may hold values from 0.099609375 to 1.8984375
- in_weight: bfloat16 [2048, 3, 2048], P('seq', None, 'tp'), may hold values from -0.125 to 0.125
- conv_weight: bfloat16 [3, 2048], P(None, 'tp'), may hold values from -3.5 to 3.5
- out_weight: bfloat16 [2048, 2048], P('tp', 'seq'), may hold values from -0.125 to 0.125
- norm_second: bfloat16 [2048], replicated, may hold values from 0.099609375 to 1.8984375
- gate_weight: bfloat16 [2048, 8192], P('seq', 'tp'), may hold values from -0.125 to 0.125
- up_weight: bfloat16 [2048, 8192], P('seq', 'tp'), may hold values from -0.125 to 0.125
- down_weight: bfloat16 [8192, 2048], P('tp', 'seq'), may hold values from -0.125 to 0.125
- out_grad: bfloat16 [8192, 2048], P('seq'), may hold values from -6 to 6
Outputs:
- block_out: bfloat16 [8192, 2048], P('seq')
- tokens_grad: float32 [8192, 2048], P('seq')
- in_grad: float32 [2048, 3, 2048], P('seq', None, 'tp')
- conv_grad: float32 [3, 2048], P(None, 'tp')
- out_proj_grad: float32 [2048, 2048], P('tp', 'seq')
- gate_grad: float32 [2048, 8192], P('seq', 'tp')
- up_grad: float32 [2048, 8192], P('seq', 'tp')
- down_grad: float32 [8192, 2048], P('tp', 'seq')
- norm_first_grad: float32 [2048], replicated
- norm_second_grad: float32 [2048], replicated
The draws below stay inside these ranges and needn't reach their ends.
Inputs may be any that keep to these rules, and one draw needn't show every extreme that they name: doc_start is 1 at row 0 and wherever a document begins.
All inputs are finite; a program needn't handle non-finite values.
Results may differ from the reference program's by a relative error of at most 0.012.
The reference program's roundings to bfloat16 on the way count: a program that leaves them out, or rounds other values in their place, can miss the bound.
Values may be sent and summed in bfloat16 or wider, within the bound.
No kernel may reach another device: no remote copies, remote signals or barrier semaphores. Data moves between devices by JAX's collectives and lax.ppermute only.
A program may use at most 256 MiB of HBM per device.

```python
import jax
import jax.numpy as jnp
from jax import lax

D = 2048
FF = 8192
TOK_DEV = 1024
TOKENS = 8192


def draw_doc_start(key, part):
    key = jax.random.fold_in(key, 11)
    key_power, key_length, key_order, key_kind = jax.random.split(key, 4)
    rows = jnp.arange(TOKENS, dtype=jnp.int32)
    power = jax.random.randint(key_power, (TOKENS,), 0, 14)
    spans = jnp.left_shift(jnp.ones((TOKENS,), jnp.int32), power)
    length = 1 + jax.random.randint(key_length, (TOKENS,), 0, 1073741824) % spans
    starts = (jnp.cumsum(length) - length).astype(jnp.int32)
    flags = jnp.zeros((TOKENS,), jnp.int32).at[starts].set(1, mode='drop')
    blocks = TOKENS // TOK_DEV
    index = jnp.arange(blocks, dtype=jnp.int32)
    guarded = (index == 1) | (index == blocks // 2) | (index == blocks - 1)
    open_slot = (index > 0) & jnp.logical_not(guarded)
    order = jax.random.permutation(key_order, blocks).astype(jnp.int32)
    priority = jnp.where(open_slot, order, -1 - index)
    chosen = lax.top_k(priority, 2)[1]
    kind = jax.random.randint(key_kind, (blocks,), 0, 3)
    kind = jnp.where(index == chosen[0], 1, jnp.where(index == chosen[1], 2, kind))
    kind = jnp.where(open_slot, kind, 0)
    block_of = rows // TOK_DEV
    offset = rows % TOK_DEV
    row_kind = kind[block_of]
    row_guard = guarded[block_of]
    next_guard = jnp.concatenate([guarded[1:], jnp.zeros((1,), jnp.bool_)])[block_of]
    clear = row_guard & (offset <= 1) | next_guard & (offset == TOK_DEV - 1) | (row_kind == 2) & (offset == 0)
    flags = jnp.where(clear, 0, flags)
    setting = (row_kind == 1) & (offset == 0) | (row_kind == 2) & (offset == 1) | (rows == 0)
    flags = jnp.where(setting, 1, flags)
    return flags.astype(jnp.int32)


def shard_levels(key, shape, cuts, least, top_value):
    def one(position, parts):
        steps = jax.random.uniform(jax.random.fold_in(jax.random.fold_in(key, 6), position), (parts,), jnp.float32, least / len(cuts), top_value / len(cuts))
        return jnp.repeat(jnp.exp(steps), shape[position] // parts).reshape((-1,) + (1,) * (len(shape) - position - 1))

    level = one(*cuts[0])
    for cut in cuts[1:]:
        level = level * one(*cut)
    return level


def centred(stream_key, extent, width, reach, shards=(), held_as=jnp.bfloat16):
    values = jax.random.normal(stream_key, extent, jnp.float32) * width
    if len(shards) > 0:
        values = shard_levels(stream_key, extent, shards, -0.22, 0.18) * values
    return jnp.clip(values, min=-reach, max=reach).astype(held_as)


def setup_inputs(seed: int = 0) -> dict:
    key_of = jax.random.split(jax.random.key(seed), 12)
    return {
        "tokens": centred(key_of[0], (TOKENS, D), 1.0, 6.0, ((0, 8),)),
        "doc_start": draw_doc_start(jax.random.fold_in(key_of[11], 71), 0),
        "norm_first": jnp.clip(1.0 + 0.18 * jax.random.normal(key_of[2], (D,), jnp.float32), 0.099609375, 1.8984375).astype(jnp.bfloat16),
        "in_weight": centred(key_of[3], (D, 3, D), D ** -0.5, 0.125, ((0, 8), (2, 4))),
        "conv_weight": centred(key_of[4], (3, D), 3 ** -0.5, 3.5, ((1, 4),)),
        "out_weight": centred(key_of[5], (D, D), D ** -0.5, 0.125, ((0, 4), (1, 8))),
        "norm_second": jnp.clip(1.0 + 0.18 * jax.random.normal(key_of[6], (D,), jnp.float32), 0.099609375, 1.8984375).astype(jnp.bfloat16),
        "gate_weight": centred(key_of[7], (D, FF), D ** -0.5, 0.125, ((0, 8), (1, 4))),
        "up_weight": centred(key_of[8], (D, FF), D ** -0.5, 0.125, ((0, 8), (1, 4))),
        "down_weight": centred(key_of[9], (FF, D), (FF // 4) ** -0.5, 0.125, ((0, 4), (1, 8))),
        "out_grad": centred(key_of[10], (TOKENS, D), 1.0, 6.0, ((0, 8),)),
    }


@jax.custom_vjp
def low(v):
    return lax.optimization_barrier(v.astype(jnp.bfloat16)).astype(jnp.float32)

@jax.custom_vjp
def low_back(v):
    return v

def low_keep(v):
    return (low(v), None)

def low_pass(kept, grad):
    return (grad,)

def back_keep(v):
    return (v, None)

def back_low(kept, grad):
    return (low(grad),)
low.defvjp(low_keep, low_pass)
low_back.defvjp(back_keep, back_low)
epsilon = 1e-05

def shift_down(field, count):
    filler = jnp.zeros((count,) + field.shape[1:], field.dtype)
    return jnp.concatenate([filler, field[:-count]], axis=0)

def rms_scale(value):
    return lax.rsqrt(lax.optimization_barrier(jnp.mean(value * value, axis=1, keepdims=True)) + epsilon)

def reference(tokens, doc_start, norm_first, in_weight, conv_weight, out_weight, norm_second, gate_weight, up_weight, down_weight, out_grad):
    kept_one = (1 - doc_start).astype(jnp.float32)[:, None]
    kept_prev = shift_down(kept_one, 1)
    highest = lax.Precision.HIGHEST

    def forward(tokens_f, gain_one, in_w, conv_w, out_w, gain_two, gate_w, up_w, down_w):
        normed_one = low(tokens_f * rms_scale(tokens_f) * gain_one)
        projected = low_back(low(jnp.einsum('td,dkc->tkc', normed_one, in_w, precision=highest)))
        left_factor = projected[:, 0]
        out_factor = projected[:, 1]
        right_factor = projected[:, 2]
        product = left_factor * right_factor
        convolved = conv_w[0] * product + conv_w[1] * kept_one * shift_down(product, 1) + conv_w[2] * kept_one * kept_prev * shift_down(product, 2)
        gated = low_back(low(out_factor * convolved))
        mixer_out = low_back(jnp.dot(gated, out_w, precision=highest))
        hidden = tokens_f + mixer_out
        normed_two = low(hidden * rms_scale(hidden) * gain_two)
        gate_val = low_back(jnp.dot(normed_two, gate_w, precision=highest))
        up_val = low_back(jnp.dot(normed_two, up_w, precision=highest))
        activated = low(jax.nn.silu(gate_val) * up_val)
        return hidden + jnp.dot(activated, down_w, precision=highest)
    inputs_f = (tokens.astype(jnp.float32), norm_first.astype(jnp.float32), in_weight.astype(jnp.float32), conv_weight.astype(jnp.float32), out_weight.astype(jnp.float32), norm_second.astype(jnp.float32), gate_weight.astype(jnp.float32), up_weight.astype(jnp.float32), down_weight.astype(jnp.float32))
    result, pullback = jax.vjp(forward, *inputs_f)
    gradients = pullback(out_grad.astype(jnp.float32))
    return (result.astype(jnp.bfloat16), gradients[0], gradients[2], gradients[3], gradients[4], gradients[6], gradients[7], gradients[8], gradients[1], gradients[5])
```

```python
import jax
import jax.numpy as jnp
from jax import lax
from jax.sharding import PartitionSpec as P

epsilon = 1e-05


def passed_along(block, axis, distance):
    devices = range(lax.axis_size(axis))
    route = [(i - distance, i) for i in devices if i - distance in devices]
    return lax.ppermute(block, axis, route)


def rms_scale(value):
    return lax.rsqrt(jnp.mean(value * value, axis=1, keepdims=True) + epsilon)


def dot_right(left, right):
    return lax.dot_general(
        left, right, (((1,), (1,)), ((), ())), preferred_element_type=jnp.float32
    )


def dot_left(left, right):
    return lax.dot_general(
        left, right, (((0,), (0,)), ((), ())), preferred_element_type=jnp.float32
    )


def norm_back(grad_normed, scaled, inverse, gain):
    weighted = grad_normed * gain
    back = inverse * (weighted - scaled * jnp.mean(weighted * scaled, axis=1, keepdims=True))
    return (back, jnp.sum(grad_normed * scaled, axis=0))


def tp_sum(part):
    return lax.psum(part.astype(jnp.bfloat16), "tp").astype(jnp.float32)


def seq_scatter(part, dim):
    narrow = part.astype(jnp.bfloat16)
    return lax.psum_scatter(narrow, "seq", scatter_dimension=dim, tiled=True).astype(jnp.float32)


def local(
    tokens,
    doc_start,
    norm_first,
    in_weight,
    conv_weight,
    out_weight,
    norm_second,
    gate_weight,
    up_weight,
    down_weight,
    out_grad,
):
    in_full, out_full, gate_full, up_full, down_full = (
        lax.all_gather(in_weight, "seq", axis=0, tiled=True),
        lax.all_gather(out_weight, "seq", axis=1, tiled=True),
        lax.all_gather(gate_weight, "seq", axis=0, tiled=True),
        lax.all_gather(up_weight, "seq", axis=0, tiled=True),
        lax.all_gather(down_weight, "seq", axis=1, tiled=True),
    )
    tokens_f = tokens.astype(jnp.float32)
    inverse_one = rms_scale(tokens_f)
    scaled_one = tokens_f * inverse_one
    gain_one = norm_first.astype(jnp.float32)
    normed_one = (scaled_one * gain_one).astype(jnp.bfloat16)
    projected = jnp.einsum(
        "td,dkc->tkc", normed_one, in_full, preferred_element_type=jnp.float32
    ).astype(jnp.bfloat16)
    left_factor = projected[:, 0].astype(jnp.float32)
    out_factor = projected[:, 1].astype(jnp.float32)
    right_factor = projected[:, 2].astype(jnp.float32)
    product = left_factor * right_factor
    kept_one = (1 - doc_start).astype(jnp.float32)[:, None]
    taps = conv_weight.astype(jnp.float32)
    tail_rows = jnp.stack([product[-1], product[-2] * kept_one[-1, 0]])
    before = passed_along(tail_rows, "seq", 1)
    previous = jnp.concatenate([before[:1], product[:-1]], axis=0)
    masked_prev = kept_one * previous
    older = jnp.concatenate([before[1:2], masked_prev[:-1]], axis=0)
    convolved = taps[0] * product + taps[1] * masked_prev + taps[2] * kept_one * older
    gated = (out_factor * convolved).astype(jnp.bfloat16)
    hidden = tokens_f + tp_sum(jnp.dot(gated, out_full, preferred_element_type=jnp.float32))
    inverse_two = rms_scale(hidden)
    scaled_two = hidden * inverse_two
    gain_two = norm_second.astype(jnp.float32)
    normed_two = (scaled_two * gain_two).astype(jnp.bfloat16)
    gate_val = jnp.dot(normed_two, gate_full, preferred_element_type=jnp.float32)
    up_val = jnp.dot(normed_two, up_full, preferred_element_type=jnp.float32)
    sigma = jax.nn.sigmoid(gate_val)
    swish = gate_val * sigma
    activated = (swish * up_val).astype(jnp.bfloat16)
    ffn_out = tp_sum(jnp.dot(activated, down_full, preferred_element_type=jnp.float32))
    result = (hidden + ffn_out).astype(jnp.bfloat16)
    grad_act = dot_right(out_grad, down_full)
    down_grad = dot_left(activated, out_grad)
    grad_gate = (grad_act * up_val * sigma * (1.0 + gate_val * (1.0 - sigma))).astype(jnp.bfloat16)
    grad_up = (grad_act * swish).astype(jnp.bfloat16)
    gate_grad = dot_left(normed_two, grad_gate)
    up_grad = dot_left(normed_two, grad_up)
    grad_normed_two = tp_sum(dot_right(grad_gate, gate_full) + dot_right(grad_up, up_full))
    grad_outside = out_grad.astype(jnp.float32)
    back_two, gain_two_grad = norm_back(grad_normed_two, scaled_two, inverse_two, gain_two)
    grad_hidden = grad_outside + back_two
    grad_mixer = grad_hidden.astype(jnp.bfloat16)
    out_proj_grad = dot_left(gated, grad_mixer)
    grad_gated = dot_right(grad_mixer, out_full).astype(jnp.bfloat16).astype(jnp.float32)
    grad_out_factor = grad_gated * convolved
    grad_conv = grad_gated * out_factor
    masked_grad = grad_conv * kept_one
    head_rows = jnp.stack([masked_grad[0], masked_grad[1] * kept_one[0, 0]])
    after = passed_along(head_rows, "seq", -1)
    next_grad = jnp.concatenate([masked_grad[1:], after[:1]], axis=0)
    folded = next_grad * kept_one
    later = jnp.concatenate([folded[1:], after[1:2]], axis=0)
    grad_product = taps[0] * grad_conv + taps[1] * next_grad + taps[2] * later
    tap_grads = jnp.stack(
        [
            jnp.sum(grad_conv * product, axis=0),
            jnp.sum(grad_conv * masked_prev, axis=0),
            jnp.sum(grad_conv * kept_one * older, axis=0),
        ]
    )
    grad_projected = jnp.stack(
        [grad_product * right_factor, grad_out_factor, grad_product * left_factor], axis=1
    ).astype(jnp.bfloat16)
    in_grad = jnp.einsum(
        "td,tkc->dkc", normed_one, grad_projected, preferred_element_type=jnp.float32
    )
    grad_normed_one = tp_sum(
        jnp.einsum("tkc,dkc->td", grad_projected, in_full, preferred_element_type=jnp.float32)
    )
    back_one, gain_one_grad = norm_back(grad_normed_one, scaled_one, inverse_one, gain_one)
    tokens_grad = grad_hidden + back_one
    gain_one_grad, gain_two_grad, tap_grads = lax.psum(
        (gain_one_grad, gain_two_grad, tap_grads), "seq"
    )
    in_grad, out_proj_grad, gate_grad, up_grad, down_grad = (
        seq_scatter(in_grad, 0),
        seq_scatter(out_proj_grad, 1),
        seq_scatter(gate_grad, 0),
        seq_scatter(up_grad, 0),
        seq_scatter(down_grad, 1),
    )
    return (
        result,
        tokens_grad,
        in_grad,
        tap_grads,
        out_proj_grad,
        gate_grad,
        up_grad,
        down_grad,
        gain_one_grad,
        gain_two_grad,
    )


def solution(mesh):
    in_specs = (
        P("seq", None),
        P("seq"),
        P(),
        P("seq", None, "tp"),
        P(None, "tp"),
        P("tp", "seq"),
        P(),
        P("seq", "tp"),
        P("seq", "tp"),
        P("tp", "seq"),
        P("seq", None),
    )
    out_specs = (
        P("seq", None),
        P("seq", None),
        P("seq", None, "tp"),
        P(None, "tp"),
        P("tp", "seq"),
        P("seq", "tp"),
        P("seq", "tp"),
        P("tp", "seq"),
        P(),
        P(),
    )
    return jax.shard_map(local, mesh=mesh, in_specs=in_specs, out_specs=out_specs, check_vma=False)
```

```python
import jax
import jax.numpy as jnp
from jax import lax
from jax.sharding import PartitionSpec as P

epsilon = 1e-05
bf16 = jnp.bfloat16
f32 = jnp.float32
halo = 16
chunks = 4


def dot_plain(left, right):
    return lax.dot_general(left, right, (((1,), (0,)), ((), ())), preferred_element_type=f32)


def dot_right(left, right):
    return lax.dot_general(left, right, (((1,), (1,)), ((), ())), preferred_element_type=f32)


def dot_left(left, right):
    return lax.dot_general(left, right, (((0,), (0,)), ((), ())), preferred_element_type=f32)


def rms_scale(value):
    return lax.rsqrt(jnp.mean(value * value, axis=1, keepdims=True) + epsilon)


def norm_back(grad_normed, scaled, inverse, gain):
    weighted = grad_normed * gain
    return inverse * (weighted - scaled * jnp.mean(weighted * scaled, axis=1, keepdims=True))


def from_before(block, axis):
    devices = lax.axis_size(axis)
    return lax.ppermute(block, axis, [(i, i + 1) for i in range(devices - 1)])


def from_after(block, axis):
    devices = lax.axis_size(axis)
    return lax.ppermute(block, axis, [(i + 1, i) for i in range(devices - 1)])


def butterfly(value, axis):
    devices = lax.axis_size(axis)
    if devices & (devices - 1):
        return lax.psum(value, axis)
    distance = 1
    while distance < devices:
        value = value + lax.ppermute(value, axis, [(i, i ^ distance) for i in range(devices)])
        distance *= 2
    return value


class Step:
    def __init__(self, name, needs, gives, run, cost, rank, lasts):
        self.name, self.needs, self.gives = name, needs, gives
        self.run, self.cost, self.rank, self.lasts = run, cost, rank, lasts


class Sum:
    def __init__(self, name, part, finish, own, joined, rank):
        self.name, self.part, self.finish = name, part, finish
        self.own, self.joined, self.rank = own, joined, rank
        self.start = None


def plan(steps, sums, line, have, budget):
    slot_of = {name: -1 for name in have}
    todo = list(steps)
    waiting = list(sums)
    taken = set()
    finishing = {}
    arriving = {}
    slots = []
    slot = 0
    while todo or waiting or any(s >= slot for s in arriving):
        for one in sorted(waiting, key=lambda q: q.rank):
            if one.part in slot_of and slot_of[one.part] < slot:
                if slot not in taken and slot + line not in taken:
                    taken.update((slot, slot + line))
                    one.start = slot
                    waiting.remove(one)
                    finishing.setdefault(slot + line - 1, []).append(one)
                    arriving.setdefault(slot + 2 * line - 1, []).append(one)
                    break
        here = []
        spent = 0.0
        for one in finishing.get(slot, []):
            slot_of[one.name + "_sum"] = slot - 1
            step = next(s for s in todo if s.name == one.finish)
            here.append(step)
            todo.remove(step)
            spent += step.cost
            slot_of.update({name: slot for name in step.gives})
        for one in arriving.get(slot, []):
            slot_of[one.joined] = slot - 1
        again = True
        while again:
            again = False
            for step in sorted(todo, key=lambda s: s.rank):
                ready = all(name in slot_of for name in step.needs)
                if ready and (spent == 0.0 or spent + step.cost <= budget):
                    here.append(step)
                    todo.remove(step)
                    spent += step.cost
                    slot_of.update({name: slot for name in step.gives})
                    again = True
                    break
        slots.append(here)
        slot += 1
    return slots


def local(
    tokens,
    doc_start,
    norm_first,
    in_weight,
    conv_weight,
    out_weight,
    norm_second,
    gate_weight,
    up_weight,
    down_weight,
    out_grad,
):
    line = lax.axis_size("tp")
    place = lax.axis_index("tp")
    count, width = tokens.shape
    rows = count // chunks
    half = rows // 2
    inner = conv_weight.shape[1]

    def tokens_of(c):
        return tokens[c * rows : (c + 1) * rows]

    def own_half(block):
        return jnp.where(place == line - 1, block[:half], block[half:])

    in_full = lax.all_gather(
        in_weight.reshape(in_weight.shape[0], 3 * inner), "seq", axis=0, tiled=True
    )
    out_full = lax.all_gather(out_weight, "seq", axis=1, tiled=True)
    gate_full = lax.all_gather(gate_weight, "seq", axis=0, tiled=True)
    up_full = lax.all_gather(up_weight, "seq", axis=0, tiled=True)
    down_full = lax.all_gather(down_weight, "seq", axis=1, tiled=True)

    gain_one = norm_first.astype(f32)
    gain_two = norm_second.astype(f32)
    taps = conv_weight.astype(f32)
    kept_one = (1 - doc_start).astype(f32)[:, None]

    def normed(block):
        value = block.astype(f32)
        return (value * rms_scale(value) * gain_one).astype(bf16)

    before_tokens = from_before(tokens[count - halo :], "seq")
    before_kept = from_before(kept_one[count - 1 :], "seq")
    normed_one = normed(tokens)
    normed_before = normed(before_tokens)

    env = {}
    kept_back = jnp.concatenate([before_kept, kept_one[:-1]], axis=0)
    both_kept = kept_one * kept_back

    def kept_of(c):
        return kept_one[c * rows : (c + 1) * rows]

    def both_of(c):
        return both_kept[c * rows : (c + 1) * rows]

    steps = []
    sums = []

    def add(name, needs, gives, cost, rank, lasts=0):
        def keep(run):
            steps.append(Step(name, needs, gives, run, cost, rank, lasts))
            return run

        return keep

    def mix(c):
        def run(e):
            block = normed_one[c * rows : (c + 1) * rows]
            if c == 0:
                block = jnp.concatenate([normed_before, block], axis=0)
            projected = dot_plain(block, in_full).astype(bf16)
            left = projected[:, :inner].astype(f32)
            right = projected[:, 2 * inner :].astype(f32)
            product = left * right
            if c == 0:
                earlier = product[halo - 2 : halo]
                product = product[halo:]
                projected = projected[halo:]
            else:
                earlier = e[f"tail{c - 1}"]
            longer = jnp.concatenate([earlier, product], axis=0)
            convolved = (
                taps[0] * product
                + taps[1] * kept_of(c) * longer[1:-1]
                + taps[2] * both_of(c) * longer[:-2]
            )
            gated = (projected[:, inner : 2 * inner].astype(f32) * convolved).astype(bf16)
            mixed = dot_plain(gated, out_full).astype(bf16)
            return projected, longer, product[-2:], convolved, gated, mixed

        needs = [] if c == 0 else [f"tail{c - 1}"]
        gives = [f"{n}{c}" for n in ("proj", "longer", "tail", "conv", "gated", "mixed")]
        add(f"mix{c}", needs, gives, 7.0, (0, c))(run)

    def first(c):
        def run(e):
            hidden = own_half(tokens_of(c)).astype(f32) + e[f"one{c}_sum"]
            inverse = rms_scale(hidden)
            return hidden, inverse, (hidden * inverse * gain_two).astype(bf16)

        add(f"first{c}", [f"one{c}_sum"], [f"hid{c}", f"inv{c}", f"n2own{c}"], 2.0, (1, c))(run)
        sums.append(Sum(f"one{c}", f"mixed{c}", f"first{c}", f"n2own{c}", f"n2{c}", (0, c)))

    def feed(c):
        def run_a(e):
            normed_two = e[f"n2{c}"]
            grads = out_grad[c * rows : (c + 1) * rows]
            gate = dot_plain(normed_two, gate_full)
            up = dot_plain(normed_two, up_full)
            grad_act = dot_right(grads, down_full)
            sig = jax.nn.sigmoid(gate)
            swish = gate * sig
            act = (swish * up).astype(bf16)
            grad_gate = (grad_act * up * sig * (1.0 + gate * (1.0 - sig))).astype(bf16)
            grad_up = (grad_act * swish).astype(bf16)
            return act, grad_gate, grad_up

        def run_b(e):
            both = dot_right(e[f"gg{c}"], gate_full) + dot_right(e[f"gu{c}"], up_full)
            return (both.astype(bf16),)

        def run_c(e):
            return (dot_plain(e[f"act{c}"], down_full).astype(bf16),)

        add(f"feedA{c}", [f"n2{c}"], [f"act{c}", f"gg{c}", f"gu{c}"], 14.0, (2, c))(run_a)
        add(f"feedB{c}", [f"gg{c}", f"gu{c}"], [f"gn2{c}"], 8.0, (2, c))(run_b)
        add(f"feedC{c}", [f"act{c}"], [f"fo{c}"], 5.0, (4, c))(run_c)

    def second(c):
        def run(e):
            hidden, inverse = e[f"hid{c}"], e[f"inv{c}"]
            scaled = hidden * inverse
            grad_normed = e[f"two{c}_sum"]
            grad_hidden = own_half(out_grad[c * rows : (c + 1) * rows]).astype(f32) + norm_back(
                grad_normed, scaled, inverse, gain_two
            )
            return grad_hidden, grad_hidden.astype(bf16), jnp.sum(grad_normed * scaled, axis=0)

        gives = [f"gh{c}", f"gmown{c}", f"g2{c}"]
        add(f"second{c}", [f"two{c}_sum", f"hid{c}", f"inv{c}"], gives, 3.0, (1, c))(run)
        sums.append(Sum(f"two{c}", f"gn2{c}", f"second{c}", f"gmown{c}", f"gm{c}", (1, c)))

    def third(c):
        def run(e):
            return ((e[f"hid{c}"] + e[f"three{c}_sum"]).astype(bf16),)

        add(f"third{c}", [f"three{c}_sum", f"hid{c}"], [f"outown{c}"], 1.0, (1, c))(run)
        sums.append(Sum(f"three{c}", f"fo{c}", f"third{c}", f"outown{c}", f"out{c}", (1.5, c)))

    def back(c):
        def run_a(e):
            grad_gated = dot_right(e[f"gm{c}"], out_full).astype(bf16).astype(f32)
            grad_conv = grad_gated * e[f"proj{c}"][:, inner : 2 * inner].astype(f32)
            grad_out = (grad_gated * e[f"conv{c}"]).astype(bf16)
            longer = e[f"longer{c}"]
            near = grad_conv * kept_of(c)
            far = grad_conv * both_of(c)
            tap_sums = jnp.stack(
                [
                    jnp.sum(grad_conv * longer[2:], axis=0),
                    jnp.sum(near * longer[1:-1], axis=0),
                    jnp.sum(far * longer[:-2], axis=0),
                ]
            )
            head = jnp.concatenate([near[:1], far[:2]], axis=0)
            passed = (from_after(head, "seq"),) if c == 0 else ()
            return (grad_conv, grad_out, tap_sums, head) + passed

        def run_b(e):
            grad_conv = e[f"gc{c}"]
            head = e[f"head{c + 1}"]
            near = jnp.concatenate([(grad_conv * kept_of(c))[1:], head[:1]], axis=0)
            far = jnp.concatenate([(grad_conv * both_of(c))[2:], head[1:]], axis=0)
            grad_product = taps[0] * grad_conv + taps[1] * near + taps[2] * far
            left = e[f"proj{c}"][:, :inner].astype(f32)
            right = e[f"proj{c}"][:, 2 * inner :].astype(f32)
            grad_projected = jnp.concatenate(
                [
                    (grad_product * right).astype(bf16),
                    e[f"go{c}"],
                    (grad_product * left).astype(bf16),
                ],
                axis=1,
            )
            return grad_projected, dot_right(grad_projected, in_full).astype(bf16)

        needs = [f"gm{c}", f"proj{c}", f"longer{c}", f"conv{c}"]
        gives = [f"gc{c}", f"go{c}", f"tap{c}", f"head{c}"]
        gives += [f"head{chunks}"] if c == 0 else []
        add(f"backA{c}", needs, gives, 5.0, (2, c))(run_a)
        needs = [f"gc{c}", f"go{c}", f"proj{c}", f"head{c + 1}"]
        add(f"backB{c}", needs, [f"gp{c}", f"gn1{c}"], 8.0, (3, c))(run_b)

    def fourth(c):
        def run(e):
            value = own_half(tokens_of(c)).astype(f32)
            inverse = rms_scale(value)
            scaled = value * inverse
            grad_normed = e[f"four{c}_sum"]
            grad_tokens = e[f"gh{c}"] + norm_back(grad_normed, scaled, inverse, gain_one)
            return grad_tokens.astype(bf16), jnp.sum(grad_normed * scaled, axis=0)

        gives = [f"gtown{c}", f"g1{c}"]
        add(f"fourth{c}", [f"four{c}_sum", f"gh{c}"], gives, 3.0, (1, c))(run)
        sums.append(Sum(f"four{c}", f"gn1{c}", f"fourth{c}", f"gtown{c}", f"gt{c}", (2, c)))

    for c in range(chunks):
        mix(c)
        first(c)
        feed(c)
        second(c)
        third(c)
        back(c)
        fourth(c)

    def joined(e, name):
        return jnp.concatenate([e[f"{name}{c}"] for c in range(chunks)], axis=0)

    def scattered(part, dim):
        return lax.psum_scatter(part.astype(bf16), "seq", scatter_dimension=dim, tiled=True)

    def names(*kinds):
        return [f"{kind}{c}" for kind in kinds for c in range(chunks)]

    add("down_grad", names("act"), ["down_grad"], 12.0, (5, 0), 6)(
        lambda e: (scattered(dot_left(joined(e, "act"), out_grad), 1),)
    )
    add("gate_grad", names("n2", "gg"), ["gate_grad"], 12.0, (5, 1), 6)(
        lambda e: (scattered(dot_left(joined(e, "n2"), joined(e, "gg")), 0),)
    )
    add("up_grad", names("n2", "gu"), ["up_grad"], 12.0, (5, 2), 6)(
        lambda e: (scattered(dot_left(joined(e, "n2"), joined(e, "gu")), 0),)
    )
    add("out_grad", names("gated", "gm"), ["out_proj_grad"], 5.0, (5, 3), 3)(
        lambda e: (scattered(dot_left(joined(e, "gated"), joined(e, "gm")), 1),)
    )
    add("in_grad", names("gp"), ["in_grad"], 10.0, (5, 4), 5)(
        lambda e: (scattered(dot_left(normed_one, joined(e, "gp")), 0),)
    )

    slots = plan(steps, sums, line, [], 16.0)
    run_slots(slots, sums, env, line, place, half)

    in_grad = env["in_grad"].astype(f32).reshape(in_weight.shape)
    out_proj_grad = env["out_proj_grad"].astype(f32)
    gate_grad = env["gate_grad"].astype(f32)
    up_grad = env["up_grad"].astype(f32)
    down_grad = env["down_grad"].astype(f32)

    def total(kind):
        return sum(env[f"{kind}{c}"] for c in range(chunks))

    owner = (place == 0) | (place == line - 1)
    gains = jnp.where(owner, jnp.stack([total("g1"), total("g2")]), 0.0)
    pieces = jnp.concatenate([gains.reshape(-1, inner), total("tap")], axis=0)
    pieces = butterfly(pieces, "seq")
    gains = butterfly(pieces[:-3], "tp").reshape(2, width)
    tap_grads = pieces[-3:]
    return (
        joined(env, "out"),
        joined(env, "gt").astype(f32),
        in_grad,
        tap_grads,
        out_proj_grad,
        gate_grad,
        up_grad,
        down_grad,
        gains[0],
        gains[1],
    )


def run_slots(slots, sums, env, line, place, half):
    up, down = {}, {}
    last = line - 1
    fresh, later, busy_until = [], {}, 0
    awaited = f"head{chunks}"

    def chosen(options):
        value = None
        for position, option in sorted(options.items(), reverse=True):
            if value is None or option is value:
                value = option
            else:
                value = jnp.where(place == position, option, value)
        return value

    for slot, steps in enumerate(slots):
        up_options, down_options = {}, {}
        for one in sums:
            if one.start is None:
                continue
            hop = slot - one.start
            if 0 <= hop < last:
                part = env[one.part]
                first, second = part[:half], part[half:]
                if hop > 0:
                    first = first + up[slot - 1]
                    second = second + down[slot - 1]
                up_options[hop] = first
                down_options[last - hop] = second
            hop = slot - one.start - line
            if 0 <= hop < last:
                up_options[hop] = env[one.own] if hop == 0 else up[slot - 1]
                down_options[last - hop] = env[one.own] if hop == 0 else down[slot - 1]
        sending = len(up_options) > 0
        for one in sums:
            if one.start is not None and slot == one.start + last:
                part = env[one.part]
                above = part[:half].astype(f32) + up[slot - 1].astype(f32)
                below = part[half:].astype(f32) + down[slot - 1].astype(f32)
                env[one.name + "_sum"] = jnp.where(place == last, above, below)
            if one.start is not None and slot == one.start + line + last:
                own, begin = env[one.own], one.start + line
                top = {last: own} | {last - 1 - j: down[begin + j] for j in range(last)}
                bottom = {0: own} | {1 + j: up[begin + j] for j in range(last)}
                env[one.joined] = jnp.concatenate([chosen(top), chosen(bottom)], axis=0)
        keys = list(fresh) + later.get(slot, [])
        for step in steps:
            keys += [name for name in step.needs if name in env and name not in keys]
        tied = [env[name] for name in keys]
        if sending:
            send_up, send_down = chosen(up_options), chosen(down_options)
            send_up, send_down, tied = lax.optimization_barrier((send_up, send_down, tied))
            up[slot] = lax.ppermute(send_up, "tp", [(p, p + 1) for p in up_options])
            down[slot] = lax.ppermute(send_down, "tp", [(p, p - 1) for p in down_options])
        elif tied:
            tied = lax.optimization_barrier(tied)
        env.update(zip(keys, tied))
        fresh = []
        for step in steps:
            env.update(zip(step.gives, step.run(env)))
            if step.lasts:
                busy_until = max(busy_until, slot + 1) + step.lasts
                later.setdefault(busy_until, []).extend(step.gives)
            else:
                fresh += [name for name in step.gives if name != awaited]


def solution(mesh):
    in_specs = (
        P("seq", None),
        P("seq"),
        P(),
        P("seq", None, "tp"),
        P(None, "tp"),
        P("tp", "seq"),
        P(),
        P("seq", "tp"),
        P("seq", "tp"),
        P("tp", "seq"),
        P("seq", None),
    )
    out_specs = (
        P("seq", None),
        P("seq", None),
        P("seq", None, "tp"),
        P(None, "tp"),
        P("tp", "seq"),
        P("seq", "tp"),
        P("seq", "tp"),
        P("tp", "seq"),
        P(),
        P(),
    )
    return jax.shard_map(local, mesh=mesh, in_specs=in_specs, out_specs=out_specs, check_vma=False)
```

```python
import functools

import jax
import jax.numpy as jnp
from jax import lax
from jax.experimental import pallas as pl
from jax.experimental.pallas import tpu as pltpu
from jax.sharding import PartitionSpec as P

epsilon = 1e-05
bf16 = jnp.bfloat16
f32 = jnp.float32
halo = 16
chunks = 4


def dot_plain(left, right):
    return lax.dot_general(left, right, (((1,), (0,)), ((), ())), preferred_element_type=f32)


def dot_right(left, right):
    return lax.dot_general(left, right, (((1,), (1,)), ((), ())), preferred_element_type=f32)


def dot_left(left, right):
    return lax.dot_general(left, right, (((0,), (0,)), ((), ())), preferred_element_type=f32)


def rms_scale(value):
    return lax.rsqrt(jnp.mean(value * value, axis=1, keepdims=True) + epsilon)


def norm_back(grad_normed, scaled, inverse, gain):
    weighted = grad_normed * gain
    return inverse * (weighted - scaled * jnp.mean(weighted * scaled, axis=1, keepdims=True))


def from_before(block, axis):
    devices = lax.axis_size(axis)
    return lax.ppermute(block, axis, [(i, i + 1) for i in range(devices - 1)])


def from_after(block, axis):
    devices = lax.axis_size(axis)
    return lax.ppermute(block, axis, [(i + 1, i) for i in range(devices - 1)])


def bits_of(axis):
    devices = lax.axis_size(axis)
    return [1 << i for i in range(devices.bit_length() - 1)]


def paired(value, axis, bit):
    return lax.ppermute(value, axis, [(i, i ^ bit) for i in range(lax.axis_size(axis))])


def place_kernel(moves, here_ref, *refs):
    pieces, out, sems = refs[:-2], refs[-2], refs[-1]
    here = here_ref[0]
    copies = []
    for number, (piece, first, size, mask, offset, dim) in enumerate(moves):
        target = pl.ds(pl.multiple_of((here ^ mask) * size, size), size)
        other = pl.ds(offset, pieces[piece].shape[1 - dim])
        if dim == 0:
            source, place = pieces[piece].at[pl.ds(first, size), :], out.at[target, other]
        else:
            source, place = pieces[piece].at[:, pl.ds(first, size)], out.at[other, target]
        copies.append(pltpu.make_async_copy(source, place, sems.at[number]))
    for copy in copies:
        copy.start()
    for copy in copies:
        copy.wait()


def placed(pieces, shape, size, dim, here):
    moves = []
    for number, (_, masks, offset) in enumerate(pieces):
        moves += [(number, size * i, size, mask, offset, dim) for i, mask in enumerate(masks)]
    anywhere = pl.BlockSpec(memory_space=pl.ANY)
    return pl.pallas_call(
        functools.partial(place_kernel, moves),
        in_specs=[pl.BlockSpec(memory_space=pltpu.SMEM)] + [anywhere] * len(pieces),
        out_specs=pl.BlockSpec(memory_space=pltpu.VMEM),
        out_shape=jax.ShapeDtypeStruct(shape, bf16),
        scratch_shapes=[pltpu.SemaphoreType.DMA((len(moves),))],
        compiler_params=pltpu.CompilerParams(vmem_limit_bytes=2 * 2**20),
        cost_estimate=pl.CostEstimate(
            flops=0, bytes_accessed=4 * shape[0] * shape[1], transcendentals=0
        ),
    )(here.reshape(1), *[piece for piece, _, _ in pieces])


class Gather:
    def __init__(self, shards, axis):
        self.shards, self.axis = shards, axis
        self.devices = lax.axis_size(axis)
        self.outer = [1 << i for i in range(1, self.devices.bit_length() - 1)]
        self.plain = self.devices & (self.devices - 1) or len(self.outer) < 2
        self.turns = 0 if self.plain else len(self.outer) + 1
        self.turn, self.held, self.pieces, self.fresh = 0, {}, {}, []
        for number, (block, dim) in enumerate(shards):
            middle = block.shape[1 - dim] // 2
            for side in range(2):
                half = lax.slice_in_dim(block, side * middle, (side + 1) * middle, axis=1 - dim)
                self.held[number, side] = [(half, [0])]
            self.pieces[number] = [(block, [0], 0)]
            self.fresh.append((number, block, [0], 0))

    def sends(self):
        values = []
        self.bits, self.notes = [], []
        if self.turn < len(self.outer):
            for (number, side), parts in self.held.items():
                block, dim = self.shards[number]
                bit = (self.outer, self.outer[::-1])[side][self.turn]
                masks = [m ^ bit for _, ms in parts for m in ms]
                blocks = [part for part, _ in parts]
                values.append(jnp.concatenate(blocks, axis=dim) if self.turn else blocks[0])
                self.bits.append(bit)
                self.notes.append((number, side, masks, side * (block.shape[1 - dim] // 2)))
        for number, value, masks, offset in self.fresh:
            values.append(value)
            self.bits.append(1)
            self.notes.append((number, None, [m ^ 1 for m in masks], offset))
        return values

    def swap(self, values):
        got = []
        for value, bit in zip(values, self.bits):
            pairs = [(i, i ^ bit) for i in range(self.devices)]
            got.append(lax.ppermute(value, self.axis, pairs))
        return got

    def take(self, got):
        self.turn += 1
        self.fresh = []
        for value, (number, side, masks, offset) in zip(got, self.notes):
            self.pieces[number].append((value, masks, offset))
            if side is not None:
                self.held[number, side].append((value, masks))
                self.fresh.append((number, value, masks, offset))

    def whole(self):
        if self.plain:
            return [lax.all_gather(b, self.axis, axis=d, tiled=True) for b, d in self.shards]
        here = lax.axis_index(self.axis)
        results = []
        for number, (block, dim) in enumerate(self.shards):
            shape = list(block.shape)
            shape[dim] *= self.devices
            results.append(placed(self.pieces[number], shape, block.shape[dim], dim, here))
        return results


def together(gathers, run=None):
    live = [gather for gather in gathers if gather.turn < gather.turns]
    sends = lax.optimization_barrier([gather.sends() for gather in live])
    got = [gather.swap(values) for gather, values in zip(live, sends)]
    extra = run() if run else ()
    got, extra = lax.optimization_barrier((got, extra))
    for gather, values in zip(live, got):
        gather.take(values)
    return extra


def feed_kernel(
    normed, grads, weights, act, grad_both, out, grad_normed, out_sum, grad_sum
):
    tile = pl.program_id(0)
    size = weights.shape[3]
    gate_w, up_w, down_w = (weights[:, i].reshape(-1, size) for i in range(3))
    gate = dot_plain(normed[...], gate_w)
    up = dot_plain(normed[...], up_w)
    grad_act = dot_plain(grads[...], down_w)
    sig = jax.nn.sigmoid(gate)
    swish = gate * sig
    act_here = (swish * up).astype(bf16)
    gate_here = (grad_act * up * sig * (1.0 + gate * (1.0 - sig))).astype(bf16)
    up_here = (grad_act * swish).astype(bf16)
    act[...] = act_here
    grad_both[0] = gate_here
    grad_both[1] = up_here
    out_here = dot_right(act_here, down_w)
    grad_here = dot_right(gate_here, gate_w) + dot_right(up_here, up_w)

    @pl.when(tile == 0)
    def _():
        out_sum[...] = out_here
        grad_sum[...] = grad_here

    @pl.when(tile > 0)
    def _():
        out_sum[...] += out_here
        grad_sum[...] += grad_here

    @pl.when(tile == pl.num_programs(0) - 1)
    def _():
        out[...] = out_sum[...].astype(bf16)
        grad_normed[...] = grad_sum[...].astype(bf16)


def feed_forward(normed, grads, weights):
    rows, width = normed.shape
    devices, _, each, hidden = weights.shape
    tile = 512 if hidden % 512 == 0 else 256
    whole = pl.BlockSpec((rows, width), lambda j: (0, 0))
    block = pl.BlockSpec((devices, 3, each, tile), lambda j: (0, 0, 0, j))
    part = pl.BlockSpec((rows, tile), lambda j: (0, j))
    both = pl.BlockSpec((2, rows, tile), lambda j: (0, 0, j))
    narrow = jax.ShapeDtypeStruct((rows, width), bf16)
    return pl.pallas_call(
        feed_kernel,
        grid=(hidden // tile,),
        in_specs=[whole, whole, block],
        out_specs=[part, both, whole, whole],
        out_shape=[
            jax.ShapeDtypeStruct((rows, hidden), bf16),
            jax.ShapeDtypeStruct((2, rows, hidden), bf16),
            narrow,
            narrow,
        ],
        scratch_shapes=[pltpu.VMEM((rows, width), f32)] * 2,
        compiler_params=pltpu.CompilerParams(vmem_limit_bytes=40 * 2**20),
        cost_estimate=pl.CostEstimate(
            flops=12 * rows * width * hidden,
            bytes_accessed=6 * width * hidden + 10 * rows * hidden,
            transcendentals=rows * hidden,
        ),
    )(normed, grads, weights)


class Step:
    def __init__(self, name, needs, gives, run, cost, rank, lasts):
        self.name, self.needs, self.gives = name, needs, gives
        self.run, self.cost, self.rank, self.lasts = run, cost, rank, lasts
        self.alone = name.startswith("small")


class Sum:
    def __init__(self, name, part, finish, own, joined, rank):
        self.name, self.part, self.finish = name, part, finish
        self.own, self.joined, self.rank = own, joined, rank
        self.start = None


def plan(steps, sums, line, budget):
    slot_of = {}
    todo = list(steps)
    waiting = list(sums)
    taken = set()
    finishing = {}
    arriving = {}
    slots = []
    slot = 0
    while todo or waiting or any(s >= slot for s in arriving):
        for one in sorted(waiting, key=lambda q: q.rank):
            if one.part in slot_of and slot_of[one.part] < slot:
                if slot not in taken and slot + line not in taken:
                    taken.update((slot, slot + line))
                    one.start = slot
                    waiting.remove(one)
                    finishing.setdefault(slot + line - 1, []).append(one)
                    arriving.setdefault(slot + 2 * line - 1, []).append(one)
                    break
        here = []
        spent = 0.0
        for one in finishing.get(slot, []):
            slot_of[one.name + "_sum"] = slot - 1
            step = next(s for s in todo if s.name == one.finish)
            here.append(step)
            todo.remove(step)
            spent += step.cost
            slot_of.update({name: slot for name in step.gives})
        for one in arriving.get(slot, []):
            slot_of[one.joined] = slot - 1
        again = True
        while again:
            again = False
            for step in sorted(todo, key=lambda s: s.rank):
                ready = all(name in slot_of for name in step.needs)
                if step.alone:
                    ready = ready and all(slot_of[name] < slot for name in step.needs)
                if not taken:
                    fits = spent + step.cost <= 7.0
                elif step.rank[0] >= 5:
                    fits = spent <= 6.0
                else:
                    fits = spent + step.cost <= budget
                if ready and (spent == 0.0 or fits):
                    here.append(step)
                    todo.remove(step)
                    spent += step.cost
                    slot_of.update({name: slot for name in step.gives})
                    again = True
                    break
        slots.append(here)
        slot += 1
    return slots


def local(
    tokens,
    doc_start,
    norm_first,
    in_weight,
    conv_weight,
    out_weight,
    norm_second,
    gate_weight,
    up_weight,
    down_weight,
    out_grad,
):
    line = lax.axis_size("tp")
    place = lax.axis_index("tp")
    count, width = tokens.shape
    rows = count // chunks
    half = rows // 2
    inner = conv_weight.shape[1]

    def tokens_of(c):
        return tokens[c * rows : (c + 1) * rows]

    def own_half(block):
        return jnp.where(place == line - 1, block[:half], block[half:])

    gain_one = norm_first.astype(f32)
    gain_two = norm_second.astype(f32)
    taps = conv_weight.astype(f32)
    kept_one = (1 - doc_start).astype(f32)[:, None]

    def normed(block):
        value = block.astype(f32)
        return (value * rms_scale(value) * gain_one).astype(bf16)

    before_tokens = from_before(tokens[count - halo :], "seq")
    before_kept = from_before(kept_one[count - 1 :], "seq")

    def norms():
        return normed(tokens), normed(before_tokens)

    def norms():
        return normed(tokens), normed(before_tokens)

    def held_back():
        return jnp.stack([gate_weight, up_weight, down_weight.T])

    in_full = lax.all_gather(
        in_weight.reshape(in_weight.shape[0], 3 * inner), "seq", axis=0, tiled=True
    )
    out_gather = Gather([(out_weight, 1)], "seq")
    feed_held = together([out_gather], held_back)
    normed_one, normed_before = together([out_gather], norms)
    while out_gather.turn < out_gather.turns:
        together([out_gather])
    (out_full,) = out_gather.whole()
    feed_full = lax.all_gather(feed_held, "seq")
    env = {}
    kept_back = jnp.concatenate([before_kept, kept_one[:-1]], axis=0)
    both_kept = kept_one * kept_back

    def kept_of(c):
        return kept_one[c * rows : (c + 1) * rows]

    def both_of(c):
        return both_kept[c * rows : (c + 1) * rows]

    steps = []
    sums = []

    def add(name, needs, gives, cost, rank, lasts=0):
        def keep(run):
            steps.append(Step(name, needs, gives, run, cost, rank, lasts))
            return run

        return keep

    def mix(c):
        def run_a(e):
            block = normed_one[c * rows : (c + 1) * rows]
            if c == 0:
                block = jnp.concatenate([normed_before, block], axis=0)
            projected = dot_plain(block, in_full).astype(bf16)
            left = projected[:, :inner].astype(f32)
            right = projected[:, 2 * inner :].astype(f32)
            product = left * right
            if c == 0:
                earlier = product[halo - 2 : halo]
                product = product[halo:]
                projected = projected[halo:]
            else:
                earlier = e[f"tail{c - 1}"]
            longer = jnp.concatenate([earlier, product], axis=0)
            convolved = (
                taps[0] * product
                + taps[1] * kept_of(c) * longer[1:-1]
                + taps[2] * both_of(c) * longer[:-2]
            )
            gated = (projected[:, inner : 2 * inner].astype(f32) * convolved).astype(bf16)
            return projected, longer, product[-2:], convolved, gated

        def run_b(e):
            return (dot_plain(e[f"gated{c}"], out_full).astype(bf16),)

        gives = [f"{n}{c}" for n in ("proj", "longer", "tail", "conv", "gated")]
        needs = [] if c == 0 else [f"tail{c - 1}"]
        add(f"mixA{c}", needs, gives, 5.0, (0, c))(run_a)
        add(f"mixB{c}", [f"gated{c}"], [f"mixed{c}"], 2.0, (0, c))(run_b)

    def first(c):
        def run(e):
            hidden = own_half(tokens_of(c)).astype(f32) + e[f"one{c}_sum"]
            inverse = rms_scale(hidden)
            return hidden, inverse, (hidden * inverse * gain_two).astype(bf16)

        add(f"first{c}", [f"one{c}_sum"], [f"hid{c}", f"inv{c}", f"n2own{c}"], 2.0, (1, c))(run)
        sums.append(Sum(f"one{c}", f"mixed{c}", f"first{c}", f"n2own{c}", f"n2{c}", (0, c)))

    def feed(c):
        def run(e):
            grads = out_grad[c * rows : (c + 1) * rows]
            return feed_forward(e[f"n2{c}"], grads, feed_full)

        gives = [f"act{c}", f"gb{c}", f"fo{c}", f"gn2{c}"]
        add(f"feed{c}", [f"n2{c}"], gives, 22.0, (2, c))(run)

    def second(c):
        def run(e):
            hidden, inverse = e[f"hid{c}"], e[f"inv{c}"]
            scaled = hidden * inverse
            grad_normed = e[f"two{c}_sum"]
            grad_hidden = own_half(out_grad[c * rows : (c + 1) * rows]).astype(f32) + norm_back(
                grad_normed, scaled, inverse, gain_two
            )
            return grad_hidden, grad_hidden.astype(bf16), jnp.sum(grad_normed * scaled, axis=0)

        gives = [f"gh{c}", f"gmown{c}", f"g2{c}"]
        add(f"second{c}", [f"two{c}_sum", f"hid{c}", f"inv{c}"], gives, 3.0, (1, c))(run)
        sums.append(Sum(f"two{c}", f"gn2{c}", f"second{c}", f"gmown{c}", f"gm{c}", (1, c)))

    def third(first, last):
        def run(e):
            blocks = []
            for c in range(first, last):
                part = e[f"fo{c}"].astype(f32)
                top = jnp.where(place == line - 1, e[f"hid{c}"], 0.0)
                bottom = jnp.where(place == 0, e[f"hid{c}"], 0.0)
                blocks += [part[:half] + top, part[half:] + bottom]
            return (lax.psum(jnp.concatenate(blocks, axis=0).astype(bf16), "tp"),)

        needs = [f"{n}{c}" for n in ("fo", "hid") for c in range(first, last)]
        add(f"third{first}", needs, [f"out{first}"], 3.0, (2.5, first), 6)(run)

    def third_line(c):
        def run(e):
            return ((e[f"hid{c}"] + e[f"three{c}_sum"]).astype(bf16),)

        add(f"third{c}", [f"three{c}_sum", f"hid{c}"], [f"outown{c}"], 1.0, (1, c))(run)
        sums.append(Sum(f"three{c}", f"fo{c}", f"third{c}", f"outown{c}", f"out{c}", (3, c)))

    def back(c):
        def run_a(e):
            grad_gated = dot_right(e[f"gm{c}"], out_full).astype(bf16).astype(f32)
            grad_conv = grad_gated * e[f"proj{c}"][:, inner : 2 * inner].astype(f32)
            grad_out = (grad_gated * e[f"conv{c}"]).astype(bf16)
            longer = e[f"longer{c}"]
            near = grad_conv * kept_of(c)
            far = grad_conv * both_of(c)
            tap_sums = jnp.stack(
                [
                    jnp.sum(grad_conv * longer[2:], axis=0),
                    jnp.sum(near * longer[1:-1], axis=0),
                    jnp.sum(far * longer[:-2], axis=0),
                ]
            )
            head = jnp.concatenate([near[:1], far[:2]], axis=0)
            passed = (from_after(head, "seq"),) if c == 0 else ()
            return (grad_conv, grad_out, tap_sums, head) + passed

        def run_b(e):
            grad_conv = e[f"gc{c}"]
            head = e[f"head{c + 1}"]
            near = jnp.concatenate([(grad_conv * kept_of(c))[1:], head[:1]], axis=0)
            far = jnp.concatenate([(grad_conv * both_of(c))[2:], head[1:]], axis=0)
            grad_product = taps[0] * grad_conv + taps[1] * near + taps[2] * far
            left = e[f"proj{c}"][:, :inner].astype(f32)
            right = e[f"proj{c}"][:, 2 * inner :].astype(f32)
            grad_projected = jnp.concatenate(
                [
                    (grad_product * right).astype(bf16),
                    e[f"go{c}"],
                    (grad_product * left).astype(bf16),
                ],
                axis=1,
            )
            grad_normed = dot_right(grad_projected, in_full).astype(bf16)
            value = tokens_of(c).astype(f32)
            gain_sum = jnp.sum(grad_normed.astype(f32) * (value * rms_scale(value)), axis=0)
            return grad_projected, grad_normed, gain_sum

        needs = [f"gm{c}", f"proj{c}", f"longer{c}", f"conv{c}"]
        gives = [f"gc{c}", f"go{c}", f"tap{c}", f"head{c}"]
        gives += [f"head{chunks}"] if c == 0 else []
        add(f"backA{c}", needs, gives, 5.0, (2, c))(run_a)
        needs = [f"gc{c}", f"go{c}", f"proj{c}", f"head{c + 1}"]
        add(f"backB{c}", needs, [f"gp{c}", f"gn1{c}", f"g1{c}"], 9.0, (3, c))(run_b)

    def fourth(c):
        def run(e):
            value = own_half(tokens_of(c)).astype(f32)
            inverse = rms_scale(value)
            scaled = value * inverse
            grad_normed = e[f"four{c}_sum"]
            grad_tokens = e[f"gh{c}"] + norm_back(grad_normed, scaled, inverse, gain_one)
            return (grad_tokens.astype(bf16),)

        add(f"fourth{c}", [f"four{c}_sum", f"gh{c}"], [f"gtown{c}"], 3.0, (1, c))(run)
        sums.append(Sum(f"four{c}", f"gn1{c}", f"fourth{c}", f"gtown{c}", f"gt{c}", (2, c)))

    for c in range(chunks):
        mix(c)
    for c in range(chunks):
        first(c)
        feed(c)
        second(c)
        back(c)
        fourth(c)

    third(0, chunks // 2)
    for c in range(chunks // 2, chunks):
        third_line(c)

    def joined(e, name):
        return jnp.concatenate([e[f"{name}{c}"] for c in range(chunks)], axis=0)

    def scattered(part, dim):
        return lax.psum_scatter(part.astype(bf16), "seq", scatter_dimension=dim, tiled=True)

    def names(*kinds):
        return [f"{kind}{c}" for kind in kinds for c in range(chunks)]

    add("down_grad", names("act"), ["down_grad"], 12.0, (5, 0), 5)(
        lambda e: (scattered(dot_left(joined(e, "act"), out_grad), 1),)
    )
    def feed_grad(e):
        both = jnp.concatenate([e[f"gb{c}"] for c in range(chunks)], axis=1)
        part = jnp.einsum("td,ktf->kdf", joined(e, "n2"), both, preferred_element_type=f32)
        return (scattered(part, 1),)

    add("feed_grad", names("n2", "gb"), ["feed_grad"], 22.0, (5, 1), 9)(feed_grad)
    add("out_grad", names("gated", "gm"), ["out_proj_grad"], 5.0, (5, 3), 3)(
        lambda e: (scattered(dot_left(joined(e, "gated"), joined(e, "gm")), 1),)
    )
    add("in_grad", names("gp"), ["in_grad"], 10.0, (5, 4), 4)(
        lambda e: (scattered(dot_left(normed_one, joined(e, "gp")), 0),)
    )

    def total(e, kind):
        return sum(e[f"{kind}{c}"] for c in range(chunks))

    def small(e):
        owner = (place == 0) | (place == line - 1)
        gains = jnp.stack([total(e, "g1"), jnp.where(owner, total(e, "g2"), 0.0)])
        return (jnp.concatenate([gains.reshape(-1, inner), total(e, "tap")], axis=0),)

    add("small", names("g1", "g2", "tap"), ["small0"], 2.0, (4, 9))(small)
    turn = 0
    for axis in ("seq", "tp"):
        for bit in bits_of(axis):

            def run(e, axis=axis, bit=bit, turn=turn):
                value = e[f"small{turn}"]
                if axis == "seq":
                    return (value + paired(value, axis, bit),)
                gains = value[:-3] + paired(value[:-3], axis, bit)
                return (jnp.concatenate([gains, value[-3:]], axis=0),)

            add(f"small{turn + 1}", [f"small{turn}"], [f"small{turn + 1}"], 2.0, (4, 10))(run)
            turn += 1

    slots = plan(steps, sums, line, 30.0)
    run_slots(slots, sums, env, line, place, half)

    in_grad = env["in_grad"].astype(f32).reshape(in_weight.shape)
    out_proj_grad = env["out_proj_grad"].astype(f32)
    gate_grad, up_grad = env["feed_grad"].astype(f32)
    down_grad = env["down_grad"].astype(f32)

    gains = env[f"small{turn}"][:-3].reshape(2, width)
    return (
        jnp.concatenate([env["out0"]] + [env[f"out{c}"] for c in range(chunks // 2, chunks)], axis=0),
        jnp.concatenate([env[f"gt{c}"].astype(f32) for c in range(chunks)], axis=0),
        in_grad,
        env[f"small{turn}"][-3:],
        out_proj_grad,
        gate_grad,
        up_grad,
        down_grad,
        gains[0],
        gains[1],
    )


def run_slots(slots, sums, env, line, place, half):
    up, down = {}, {}
    last = line - 1
    fresh, later, busy_until = [], {}, 0
    awaited = f"head{chunks}"

    def chosen(options):
        value = None
        for position, option in sorted(options.items(), reverse=True):
            if value is None or option is value:
                value = option
            else:
                value = jnp.where(place == position, option, value)
        return value

    def local_parts(slot):
        up_options, down_options = {}, {}
        for one in sums:
            if one.start is None:
                continue
            hop = slot - one.start
            if 0 <= hop < last:
                part = env[one.part]
                up_options[hop] = part[:half]
                down_options[last - hop] = part[half:]
            hop = slot - one.start - line
            if 0 <= hop < last:
                value = env[one.own] if hop == 0 else None
                up_options[hop] = down_options[last - hop] = value
        return up_options, down_options

    def mixed(options):
        if all(value is None for value in options.values()):
            return None
        return chosen({p: 0.0 if value is None else value for p, value in options.items()})

    ready = None
    for slot, steps in enumerate(slots):
        up_options, down_options = local_parts(slot)
        sending = len(up_options) > 0
        if sending:
            send_up, send_down = ready if ready is not None else (None, None)
            if ready is None:
                send_up, send_down = mixed(up_options), mixed(down_options)
            if slot - 1 in up:
                send_up = up[slot - 1] if send_up is None else send_up + up[slot - 1]
                send_down = down[slot - 1] if send_down is None else send_down + down[slot - 1]
        for one in sums:
            if one.start is not None and slot == one.start + last:
                part = env[one.part]
                above = part[:half].astype(f32) + up[slot - 1].astype(f32)
                below = part[half:].astype(f32) + down[slot - 1].astype(f32)
                env[one.name + "_sum"] = jnp.where(place == last, above, below)
            if one.start is not None and slot == one.start + line + last:
                own, begin = env[one.own], one.start + line
                top = {last: own} | {last - 1 - j: down[begin + j] for j in range(last)}
                bottom = {0: own} | {1 + j: up[begin + j] for j in range(last)}
                env[one.joined] = jnp.concatenate([chosen(top), chosen(bottom)], axis=0)
        keys = list(fresh) + later.get(slot, [])
        for step in steps:
            keys += [name for name in step.needs if name in env and name not in keys]
        tied = [env[name] for name in keys]
        if sending:
            send_up, send_down, tied = lax.optimization_barrier((send_up, send_down, tied))
            up[slot] = lax.ppermute(send_up, "tp", [(p, p + 1) for p in up_options])
            down[slot] = lax.ppermute(send_down, "tp", [(p, p - 1) for p in down_options])
        elif tied:
            tied = lax.optimization_barrier(tied)
        env.update(zip(keys, tied))
        fresh = []
        for step in steps:
            env.update(zip(step.gives, step.run(env)))
            if step.lasts:
                busy_until = max(busy_until, slot + 1) + step.lasts
                later.setdefault(busy_until, []).extend(step.gives)
            else:
                fresh += [name for name in step.gives if name != awaited]
        ready = tuple(mixed(options) for options in local_parts(slot + 1))


def solution(mesh):
    in_specs = (
        P("seq", None),
        P("seq"),
        P(),
        P("seq", None, "tp"),
        P(None, "tp"),
        P("tp", "seq"),
        P(),
        P("seq", "tp"),
        P("seq", "tp"),
        P("tp", "seq"),
        P("seq", None),
    )
    out_specs = (
        P("seq", None),
        P("seq", None),
        P("seq", None, "tp"),
        P(None, "tp"),
        P("tp", "seq"),
        P("seq", "tp"),
        P("seq", "tp"),
        P("tp", "seq"),
        P(),
        P(),
    )
    return jax.shard_map(local, mesh=mesh, in_specs=in_specs, out_specs=out_specs, check_vma=False)
```

```python
import functools

import jax
import jax.numpy as jnp
from jax import lax
from jax.experimental import pallas as pl
from jax.experimental.pallas import tpu as pltpu
from jax.sharding import PartitionSpec as P

epsilon = 1e-05
bf16 = jnp.bfloat16
f32 = jnp.float32
halo = 16
chunks = 4


def dot_plain(left, right):
    return lax.dot_general(left, right, (((1,), (0,)), ((), ())), preferred_element_type=f32)


def dot_right(left, right):
    return lax.dot_general(left, right, (((1,), (1,)), ((), ())), preferred_element_type=f32)


def dot_left(left, right):
    return lax.dot_general(left, right, (((0,), (0,)), ((), ())), preferred_element_type=f32)


def rms_scale(value):
    return lax.rsqrt(jnp.mean(value * value, axis=1, keepdims=True) + epsilon)


def norm_back(grad_normed, scaled, inverse, gain):
    weighted = grad_normed * gain
    return inverse * (weighted - scaled * jnp.mean(weighted * scaled, axis=1, keepdims=True))


def from_before(block, axis):
    devices = lax.axis_size(axis)
    return lax.ppermute(block, axis, [(i, i + 1) for i in range(devices - 1)])


def from_after(block, axis):
    devices = lax.axis_size(axis)
    return lax.ppermute(block, axis, [(i + 1, i) for i in range(devices - 1)])


def bits_of(axis):
    devices = lax.axis_size(axis)
    return [1 << i for i in range(devices.bit_length() - 1)]


def paired(value, axis, bit):
    return lax.ppermute(value, axis, [(i, i ^ bit) for i in range(lax.axis_size(axis))])


def place_kernel(moves, here_ref, *refs):
    pieces, out, sems = refs[:-2], refs[-2], refs[-1]
    here = here_ref[0]
    copies = []
    for number, (piece, first, size, mask, offset, dim) in enumerate(moves):
        target = pl.ds(pl.multiple_of((here ^ mask) * size, size), size)
        other = pl.ds(offset, pieces[piece].shape[1 - dim])
        if dim == 0:
            source, place = pieces[piece].at[pl.ds(first, size), :], out.at[target, other]
        else:
            source, place = pieces[piece].at[:, pl.ds(first, size)], out.at[other, target]
        copies.append(pltpu.make_async_copy(source, place, sems.at[number]))
    for copy in copies:
        copy.start()
    for copy in copies:
        copy.wait()


def placed(pieces, shape, size, dim, here):
    moves = []
    for number, (_, masks, offset) in enumerate(pieces):
        moves += [(number, size * i, size, mask, offset, dim) for i, mask in enumerate(masks)]
    anywhere = pl.BlockSpec(memory_space=pl.ANY)
    return pl.pallas_call(
        functools.partial(place_kernel, moves),
        in_specs=[pl.BlockSpec(memory_space=pltpu.SMEM)] + [anywhere] * len(pieces),
        out_specs=pl.BlockSpec(memory_space=pltpu.VMEM),
        out_shape=jax.ShapeDtypeStruct(shape, bf16),
        scratch_shapes=[pltpu.SemaphoreType.DMA((len(moves),))],
        compiler_params=pltpu.CompilerParams(vmem_limit_bytes=2 * 2**20),
        cost_estimate=pl.CostEstimate(
            flops=0, bytes_accessed=4 * shape[0] * shape[1], transcendentals=0
        ),
    )(here.reshape(1), *[piece for piece, _, _ in pieces])


class Gather:
    def __init__(self, shards, axis):
        self.shards, self.axis = shards, axis
        self.devices = lax.axis_size(axis)
        self.outer = [1 << i for i in range(1, self.devices.bit_length() - 1)]
        self.plain = self.devices & (self.devices - 1) or len(self.outer) < 2
        self.turns = 0 if self.plain else len(self.outer) + 1
        self.turn, self.held, self.pieces, self.fresh = 0, {}, {}, []
        for number, (block, dim) in enumerate(shards):
            middle = block.shape[1 - dim] // 2
            for side in range(2):
                half = lax.slice_in_dim(block, side * middle, (side + 1) * middle, axis=1 - dim)
                self.held[number, side] = [(half, [0])]
            self.pieces[number] = [(block, [0], 0)]
            self.fresh.append((number, block, [0], 0))

    def sends(self):
        values = []
        self.bits, self.notes = [], []
        if self.turn < len(self.outer):
            for (number, side), parts in self.held.items():
                block, dim = self.shards[number]
                bit = (self.outer, self.outer[::-1])[side][self.turn]
                masks = [m ^ bit for _, ms in parts for m in ms]
                blocks = [part for part, _ in parts]
                values.append(jnp.concatenate(blocks, axis=dim) if self.turn else blocks[0])
                self.bits.append(bit)
                self.notes.append((number, side, masks, side * (block.shape[1 - dim] // 2)))
        for number, value, masks, offset in self.fresh:
            values.append(value)
            self.bits.append(1)
            self.notes.append((number, None, [m ^ 1 for m in masks], offset))
        return values

    def swap(self, values):
        got = []
        for value, bit in zip(values, self.bits):
            pairs = [(i, i ^ bit) for i in range(self.devices)]
            got.append(lax.ppermute(value, self.axis, pairs))
        return got

    def take(self, got):
        self.turn += 1
        self.fresh = []
        for value, (number, side, masks, offset) in zip(got, self.notes):
            self.pieces[number].append((value, masks, offset))
            if side is not None:
                self.held[number, side].append((value, masks))
                self.fresh.append((number, value, masks, offset))

    def whole(self):
        if self.plain:
            return [lax.all_gather(b, self.axis, axis=d, tiled=True) for b, d in self.shards]
        here = lax.axis_index(self.axis)
        results = []
        for number, (block, dim) in enumerate(self.shards):
            shape = list(block.shape)
            shape[dim] *= self.devices
            results.append(placed(self.pieces[number], shape, block.shape[dim], dim, here))
        return results


def together(gathers, run=None):
    live = [gather for gather in gathers if gather.turn < gather.turns]
    sends = lax.optimization_barrier([gather.sends() for gather in live])
    got = [gather.swap(values) for gather, values in zip(live, sends)]
    extra = run() if run else ()
    got, extra = lax.optimization_barrier((got, extra))
    for gather, values in zip(live, got):
        gather.take(values)
    return extra


def light(elements):
    return pl.CostEstimate(flops=elements, bytes_accessed=elements, transcendentals=0)


def feed_kernel(
    normed, grads, weights, act, grad_gate, grad_up, out, grad_normed, out_sum, grad_sum
):
    tile = pl.program_id(0)
    size = weights.shape[3]
    gate_w, up_w, down_w = (weights[:, i].reshape(-1, size) for i in range(3))
    gate = dot_plain(normed[...], gate_w)
    up = dot_plain(normed[...], up_w)
    grad_act = dot_plain(grads[...], down_w)
    sig = jax.nn.sigmoid(gate)
    swish = gate * sig
    act_here = (swish * up).astype(bf16)
    gate_here = (grad_act * up * sig * (1.0 + gate * (1.0 - sig))).astype(bf16)
    up_here = (grad_act * swish).astype(bf16)
    act[...] = act_here
    grad_gate[...] = gate_here
    grad_up[...] = up_here
    out_here = dot_right(act_here, down_w)
    grad_here = dot_right(gate_here, gate_w) + dot_right(up_here, up_w)

    @pl.when(tile == 0)
    def _():
        out_sum[...] = out_here
        grad_sum[...] = grad_here

    @pl.when(tile > 0)
    def _():
        out_sum[...] += out_here
        grad_sum[...] += grad_here

    @pl.when(tile == pl.num_programs(0) - 1)
    def _():
        out[...] = out_sum[...].astype(bf16)
        grad_normed[...] = grad_sum[...].astype(bf16)


def feed_forward(normed, grads, weights):
    rows, width = normed.shape
    devices, _, each, hidden = weights.shape
    tile = 512 if hidden % 512 == 0 else 256
    whole = pl.BlockSpec((rows, width), lambda j: (0, 0))
    block = pl.BlockSpec((devices, 3, each, tile), lambda j: (0, 0, 0, j))
    part = pl.BlockSpec((rows, tile), lambda j: (0, j))
    wide = jax.ShapeDtypeStruct((rows, hidden), bf16)
    narrow = jax.ShapeDtypeStruct((rows, width), bf16)
    return pl.pallas_call(
        feed_kernel,
        grid=(hidden // tile,),
        in_specs=[whole, whole, block],
        out_specs=[part, part, part, whole, whole],
        out_shape=[
            wide,
            wide,
            wide,
            narrow,
            narrow,
        ],
        scratch_shapes=[pltpu.VMEM((rows, width), f32)] * 2,
        compiler_params=pltpu.CompilerParams(vmem_limit_bytes=36 * 2**20),
        cost_estimate=pl.CostEstimate(
            flops=12 * rows * width * hidden,
            bytes_accessed=6 * width * hidden + 10 * rows * hidden,
            transcendentals=rows * hidden,
        ),
    )(normed, grads, weights)


def mixer_kernel(left, right, left_last, right_last, out):
    last = pl.num_programs(0) - 1

    @pl.when(pl.program_id(0) < last)
    def _():
        out[...] = dot_left(left[...], right[...]).astype(bf16)

    @pl.when(pl.program_id(0) == last)
    def _():
        out[...] = dot_left(left_last[...], right_last[...]).astype(bf16)


def mixer_products(left, right, left_last, right_last):
    count, width = left.shape
    tile = right_last.shape[1]
    tiles = right.shape[1] // tile
    whole = pl.BlockSpec((count, width), lambda j: (0, 0), pipeline_mode=pl.Buffered(1))
    return pl.pallas_call(
        mixer_kernel,
        grid=(tiles + 1,),
        in_specs=[
            whole,
            pl.BlockSpec((count, tile), lambda j: (0, jnp.minimum(j, tiles - 1))),
            whole,
            pl.BlockSpec((count, tile), lambda j: (0, 0)),
        ],
        out_specs=pl.BlockSpec((width, tile), lambda j: (0, j)),
        out_shape=jax.ShapeDtypeStruct((width, (tiles + 1) * tile), bf16),
        compiler_params=pltpu.CompilerParams(vmem_limit_bytes=24 * 2**20),
        cost_estimate=light(count * tile),
    )(left, right, left_last, right_last)


class Step:
    def __init__(self, name, needs, gives, run, cost, rank, lasts):
        self.name, self.needs, self.gives = name, needs, gives
        self.run, self.cost, self.rank, self.lasts = run, cost, rank, lasts
        self.alone = name.startswith(("small", "call"))


class Sum:
    def __init__(self, name, part, finish, own, joined, rank, back_rank):
        self.name, self.part, self.finish = name, part, finish
        self.own, self.joined, self.rank, self.back_rank = own, joined, rank, back_rank
        self.start = self.back = None


def plan(steps, sums, line, budget):
    slot_of = {}
    todo = list(steps)
    waiting = list(sums)
    finishing, returning, arriving = {}, [], {}
    slots = []
    slot = busy = 0
    while todo or waiting or returning or any(s >= slot for s in arriving):
        ready = [one for one in waiting if slot_of.get(one.part, slot) < slot]
        back = [one for one in returning if slot >= one.start + line]
        turn = [(one.rank, one) for one in ready] + [(one.back_rank, one) for one in back]
        if turn:
            one = min(turn, key=lambda t: t[0])[1]
            if one in ready:
                one.start = slot
                waiting.remove(one)
                returning.append(one)
                finishing.setdefault(slot + line - 1, []).append(one)
            else:
                one.back = slot
                returning.remove(one)
                arriving.setdefault(slot + line - 1, []).append(one)
        here = []
        spent = 0.0
        for one in finishing.get(slot, []):
            slot_of[one.name + "_sum"] = slot - 1
            step = next(s for s in todo if s.name == one.finish)
            here.append(step)
            todo.remove(step)
            spent += step.cost
            slot_of.update({name: slot for name in step.gives})
        for one in arriving.get(slot, []):
            slot_of[one.joined] = slot - 1
        again = True
        while again:
            again = False
            for step in sorted(todo, key=lambda s: s.rank):
                newest = max((slot_of.get(name, slot + 1) for name in step.needs), default=-1)
                ready = newest < slot if step.alone else newest <= slot
                if len(waiting) == len(sums):
                    fits = spent + step.cost <= 7.0
                elif step.rank[0] >= 5:
                    fits = spent <= 6.0 or spent + step.cost <= budget
                else:
                    fits = spent + step.cost <= budget or step.cost <= 3.0
                    fits = fits or (spent <= 4.0 and step.cost > budget)
                if ready and (spent == 0.0 or fits):
                    here.append(step)
                    todo.remove(step)
                    spent += step.cost
                    if step.lasts:
                        step.until = busy = max(busy, slot + 1) + step.lasts
                    until = step.until if step.lasts else slot
                    slot_of.update({name: until for name in step.gives})
                    again = True
                    break
        slots.append(here)
        slot += 1
    return slots


def local(
    tokens,
    doc_start,
    norm_first,
    in_weight,
    conv_weight,
    out_weight,
    norm_second,
    gate_weight,
    up_weight,
    down_weight,
    out_grad,
):
    line = lax.axis_size("tp")
    place = lax.axis_index("tp")
    count, width = tokens.shape
    rows = count // chunks
    half = rows // 2
    inner = conv_weight.shape[1]

    def tokens_of(c):
        return tokens[c * rows : (c + 1) * rows]

    def own_half(block):
        return jnp.where(place == line - 1, block[:half], block[half:])

    gain_one = norm_first.astype(f32)
    gain_two = norm_second.astype(f32)
    taps = conv_weight.astype(f32)
    kept_one = (1 - doc_start).astype(f32)[:, None]

    def normed(block):
        value = block.astype(f32)
        return (value * rms_scale(value) * gain_one).astype(bf16)

    before_tokens = from_before(tokens[count - halo :], "seq")
    before_kept = from_before(kept_one[count - 1 :], "seq")

    def norms():
        return normed(tokens), normed(before_tokens)

    def norms():
        return normed(tokens), normed(before_tokens)

    def held_back():
        return jnp.stack([gate_weight, up_weight, down_weight.T])

    in_full = lax.all_gather(
        in_weight.reshape(in_weight.shape[0], 3 * inner), "seq", axis=0, tiled=True
    )
    out_gather = Gather([(out_weight, 1)], "seq")
    feed_held = together([out_gather], held_back)
    normed_one, normed_before = together([out_gather], norms)
    while out_gather.turn < out_gather.turns:
        together([out_gather])
    (out_full,) = out_gather.whole()
    feed_full = lax.all_gather(feed_held, "seq")
    env = {}
    kept_back = jnp.concatenate([before_kept, kept_one[:-1]], axis=0)
    both_kept = kept_one * kept_back

    def kept_of(c):
        return kept_one[c * rows : (c + 1) * rows]

    def both_of(c):
        return both_kept[c * rows : (c + 1) * rows]

    steps = []
    sums = []

    def add(name, needs, gives, cost, rank, lasts=0):
        def keep(run):
            steps.append(Step(name, needs, gives, run, cost, rank, lasts))
            return run

        return keep

    def mix(c):
        def run_a(e):
            block = normed_one[c * rows : (c + 1) * rows]
            if c == 0:
                block = jnp.concatenate([normed_before, block], axis=0)
            projected = dot_plain(block, in_full).astype(bf16)
            left = projected[:, :inner].astype(f32)
            right = projected[:, 2 * inner :].astype(f32)
            product = left * right
            if c == 0:
                earlier = product[halo - 2 : halo]
                product = product[halo:]
                projected = projected[halo:]
            else:
                earlier = e[f"tail{c - 1}"]
            longer = jnp.concatenate([earlier, product], axis=0)
            convolved = (
                taps[0] * product
                + taps[1] * kept_of(c) * longer[1:-1]
                + taps[2] * both_of(c) * longer[:-2]
            )
            gated = (projected[:, inner : 2 * inner].astype(f32) * convolved).astype(bf16)
            return projected, longer, product[-2:], convolved, gated

        def run_b(e):
            return (dot_plain(e[f"gated{c}"], out_full).astype(bf16),)

        gives = [f"{n}{c}" for n in ("proj", "longer", "tail", "conv", "gated")]
        needs = [] if c == 0 else [f"tail{c - 1}"]
        add(f"mixA{c}", needs, gives, 5.0, (0, c))(run_a)
        add(f"mixB{c}", [f"gated{c}"], [f"mixed{c}"], 2.0, (0, c))(run_b)

    def first(c):
        def run(e):
            hidden = own_half(tokens_of(c)).astype(f32) + e[f"one{c}_sum"]
            inverse = rms_scale(hidden)
            return hidden, inverse, (hidden * inverse * gain_two).astype(bf16)

        add(f"first{c}", [f"one{c}_sum"], [f"hid{c}", f"inv{c}", f"n2own{c}"], 2.0, (1, c))(run)
        sums.append(Sum(f"one{c}", f"mixed{c}", f"first{c}", f"n2own{c}", f"n2{c}", (0, c), (0.5, c)))

    def feed(c):
        def run(e):
            grads = out_grad[c * rows : (c + 1) * rows]
            return feed_forward(e[f"n2{c}"], grads, feed_full)

        gives = [f"act{c}", f"gg{c}", f"gu{c}", f"fo{c}", f"gn2{c}"]
        add(f"feed{c}", [f"n2{c}"], gives, 22.0, (2, c))(run)

    def second(c):
        def run(e):
            hidden, inverse = e[f"hid{c}"], e[f"inv{c}"]
            scaled = hidden * inverse
            grad_normed = e[f"two{c}_sum"]
            grad_hidden = own_half(out_grad[c * rows : (c + 1) * rows]).astype(f32) + norm_back(
                grad_normed, scaled, inverse, gain_two
            )
            return grad_hidden, grad_hidden.astype(bf16), jnp.sum(grad_normed * scaled, axis=0)

        gives = [f"gh{c}", f"gmown{c}", f"g2{c}"]
        add(f"second{c}", [f"two{c}_sum", f"hid{c}", f"inv{c}"], gives, 3.0, (1, c))(run)
        sums.append(Sum(f"two{c}", f"gn2{c}", f"second{c}", f"gmown{c}", f"gm{c}", (1, c), (1.5, c)))

    def third(last):
        def run_part(e):
            blocks = []
            for c in range(last):
                part = e[f"fo{c}"].astype(f32)
                top = jnp.where(place == line - 1, e[f"hid{c}"], 0.0)
                bottom = jnp.where(place == 0, e[f"hid{c}"], 0.0)
                blocks += [part[:half] + top, part[half:] + bottom]
            return (lax.psum(jnp.concatenate(blocks, axis=0).astype(bf16), "tp"),)

        needs = [f"{n}{c}" for n in ("fo", "hid") for c in range(last)]
        add("third0", needs, ["out0"], 3.0, (2.5, 0), 5)(run_part)

    def third_line(c):
        def run(e):
            return ((e[f"hid{c}"] + e[f"three{c}_sum"]).astype(bf16),)

        add(f"third{c}", [f"three{c}_sum", f"hid{c}"], [f"outown{c}"], 1.0, (1, c))(run)
        sums.append(Sum(f"three{c}", f"fo{c}", f"third{c}", f"outown{c}", f"out{c}", (3, c), (5, c)))

    def back(c):
        def run_a(e):
            grad_gated = dot_right(e[f"gm{c}"], out_full).astype(bf16).astype(f32)
            grad_conv = grad_gated * e[f"proj{c}"][:, inner : 2 * inner].astype(f32)
            grad_out = (grad_gated * e[f"conv{c}"]).astype(bf16)
            longer = e[f"longer{c}"]
            near = grad_conv * kept_of(c)
            far = grad_conv * both_of(c)
            tap_sums = jnp.stack(
                [
                    jnp.sum(grad_conv * longer[2:], axis=0),
                    jnp.sum(near * longer[1:-1], axis=0),
                    jnp.sum(far * longer[:-2], axis=0),
                ]
            )
            head = jnp.concatenate([near[:1], far[:2]], axis=0)
            passed = (from_after(head, "seq"),) if c == 0 else ()
            return (grad_conv, grad_out, tap_sums, head) + passed

        def run_b(e):
            grad_conv = e[f"gc{c}"]
            head = e[f"head{c + 1}"]
            near = jnp.concatenate([(grad_conv * kept_of(c))[1:], head[:1]], axis=0)
            far = jnp.concatenate([(grad_conv * both_of(c))[2:], head[1:]], axis=0)
            grad_product = taps[0] * grad_conv + taps[1] * near + taps[2] * far
            left = e[f"proj{c}"][:, :inner].astype(f32)
            right = e[f"proj{c}"][:, 2 * inner :].astype(f32)
            grad_projected = jnp.concatenate(
                [
                    (grad_product * right).astype(bf16),
                    e[f"go{c}"],
                    (grad_product * left).astype(bf16),
                ],
                axis=1,
            )
            grad_normed = dot_right(grad_projected, in_full).astype(bf16)
            value = tokens_of(c).astype(f32)
            gain_sum = jnp.sum(grad_normed.astype(f32) * (value * rms_scale(value)), axis=0)
            return grad_projected, grad_normed, gain_sum

        needs = [f"gm{c}", f"proj{c}", f"longer{c}", f"conv{c}"]
        gives = [f"gc{c}", f"go{c}", f"tap{c}", f"head{c}"]
        gives += [f"head{chunks}"] if c == 0 else []
        add(f"backA{c}", needs, gives, 5.0, (2, c))(run_a)
        needs = [f"gc{c}", f"go{c}", f"proj{c}", f"head{c + 1}"]
        add(f"backB{c}", needs, [f"gp{c}", f"gn1{c}", f"g1{c}"], 9.0, (3, c))(run_b)

    def fourth(c):
        def run(e):
            value = own_half(tokens_of(c)).astype(f32)
            inverse = rms_scale(value)
            scaled = value * inverse
            grad_normed = e[f"four{c}_sum"]
            grad_tokens = e[f"gh{c}"] + norm_back(grad_normed, scaled, inverse, gain_one)
            return (grad_tokens.astype(bf16),)

        add(f"fourth{c}", [f"four{c}_sum", f"gh{c}"], [f"gtown{c}"], 3.0, (1, c))(run)
        sums.append(Sum(f"four{c}", f"gn1{c}", f"fourth{c}", f"gtown{c}", f"gt{c}", (2, c), (4, c)))

    for c in range(chunks):
        mix(c)
    for c in range(chunks):
        first(c)
        feed(c)
        second(c)
        back(c)
        fourth(c)

    third(chunks // 2)
    for c in range(chunks // 2, chunks):
        third_line(c)

    def joined(e, name):
        return jnp.concatenate([e[f"{name}{c}"] for c in range(chunks)], axis=0)

    def names(*kinds):
        return [f"{kind}{c}" for kind in kinds for c in range(chunks)]

    def scattered_sum(name, needs, run, cost, order, dim, lasts):
        add(f"{name}_part", needs, [f"{name}_part"], cost, (5, order))(run)

        def call(e):
            return (lax.psum_scatter(e[f"{name}_part"], "seq", scatter_dimension=dim, tiled=True),)

        add(f"call_{name}", [f"{name}_part"], [name], 0.0, (2.6, 9 + order), lasts)(call)

    def down_part(e):
        return (dot_left(joined(e, "act"), out_grad).astype(bf16),)

    def gate_part(e):
        return (dot_left(joined(e, "n2"), joined(e, "gg")).astype(bf16),)

    def up_part(e):
        return (dot_left(joined(e, "n2"), joined(e, "gu")).astype(bf16),)

    def mixer_part(e):
        return (mixer_products(normed_one, joined(e, "gp"), joined(e, "gm"), joined(e, "gated")),)

    scattered_sum("down_grad", names("act"), down_part, 12.0, 0, 1, 4)
    scattered_sum("gate_grad", names("n2", "gg"), gate_part, 11.0, 1, 0, 4)
    scattered_sum("up_grad", names("n2", "gu"), up_part, 11.0, 1.5, 0, 4)
    scattered_sum("mixer_grad", names("gm", "gated", "gp"), mixer_part, 18.0, 2, 0, 4)

    def total(e, kind):
        return sum(e[f"{kind}{c}"] for c in range(chunks))

    def small(e):
        owner = (place == 0) | (place == line - 1)
        gains = jnp.stack([total(e, "g1"), jnp.where(owner, total(e, "g2"), 0.0)])
        return (jnp.concatenate([gains.reshape(-1, inner), total(e, "tap")], axis=0),)

    add("small", names("g1", "g2", "tap"), ["small0"], 2.0, (4, 9))(small)
    turn = 0
    for axis in ("seq", "tp"):
        for bit in bits_of(axis):

            def run(e, axis=axis, bit=bit, turn=turn):
                value = e[f"small{turn}"]
                if axis == "seq":
                    return (value + paired(value, axis, bit),)
                gains = value[:-3] + paired(value[:-3], axis, bit)
                return (jnp.concatenate([gains, value[-3:]], axis=0),)

            add(f"small{turn + 1}", [f"small{turn}"], [f"small{turn + 1}"], 2.0, (4, 10))(run)
            turn += 1

    def rows_put(name, needs, first, step):
        def run(e):
            block = e[needs[0]].astype(f32 if name == "tokens_grad" else bf16)
            if len(needs) == 1:
                return (jnp.pad(block, ((0, count - block.shape[0]), (0, 0))),)
            return (lax.dynamic_update_slice(e[needs[1]], block, (first, 0)),)

        add(f"{name}_{step}", needs, [f"{name}{step}"], 2.0, (4.6, step))(run)

    for c in range(chunks):
        so_far = [f"tokens_grad{c - 1}"] if c else []
        rows_put("tokens_grad", [f"gt{c}"] + so_far, c * rows, c)
    rows_put("block_out", ["out0"], 0, 0)
    for c in range(chunks // 2, chunks):
        step = c - chunks // 2 + 1
        rows_put("block_out", [f"out{c}", f"block_out{step - 1}"], c * rows, step)

    def widened(name):
        add(f"{name}_wide", [f"{name}_grad"], [f"{name}_wide"], 2.0, (4.7, 0))(
            lambda e: (e[f"{name}_grad"].astype(f32),)
        )

    for name in ("down", "gate", "up"):
        widened(name)

    def mixer_wide(e):
        mixer_grad = e["mixer_grad"].astype(f32)
        return mixer_grad[:, : 3 * inner].reshape(in_weight.shape), mixer_grad[:, 3 * inner :].T

    add("mixer_wide", ["mixer_grad"], ["in_wide", "out_wide"], 3.0, (4.7, 1))(mixer_wide)

    slots = plan(steps, sums, line, 16.0)
    run_slots(slots, sums, env, line, place, half)

    gains = env[f"small{turn}"][:-3].reshape(2, width)
    return (
        env[f"block_out{chunks - chunks // 2}"],
        env[f"tokens_grad{chunks - 1}"],
        env["in_wide"],
        env[f"small{turn}"][-3:],
        env["out_wide"],
        env["gate_wide"],
        env["up_wide"],
        env["down_wide"],
        gains[0],
        gains[1],
    )


def run_slots(slots, sums, env, line, place, half):
    up, down = {}, {}
    last = line - 1
    fresh, later = [], {}
    awaited = f"head{chunks}"

    def chosen(options):
        value = None
        for position, option in sorted(options.items(), reverse=True):
            if value is None or option is value:
                value = option
            else:
                value = jnp.where(place == position, option, value)
        return value

    def local_parts(slot):
        up_options, down_options = {}, {}
        for one in sums:
            hop = slot - one.start
            if 0 <= hop < last:
                part = env[one.part]
                up_options[hop] = part[:half]
                down_options[last - hop] = part[half:]
            hop = slot - one.back
            if 0 <= hop < last:
                value = env[one.own] if hop == 0 else None
                up_options[hop] = down_options[last - hop] = value
        return up_options, down_options

    def mixed(options):
        if all(value is None for value in options.values()):
            return None
        return chosen({p: 0.0 if value is None else value for p, value in options.items()})

    ready = None
    for slot, steps in enumerate(slots):
        up_options, down_options = local_parts(slot)
        sending = len(up_options) > 0
        if sending:
            send_up, send_down = ready if ready is not None else (None, None)
            if ready is None:
                send_up, send_down = mixed(up_options), mixed(down_options)
            if slot - 1 in up:
                send_up = up[slot - 1] if send_up is None else send_up + up[slot - 1]
                send_down = down[slot - 1] if send_down is None else send_down + down[slot - 1]
        for one in sums:
            if slot == one.back + last:
                own, begin = env[one.own], one.back
                top = {last: own} | {last - 1 - j: down[begin + j] for j in range(last)}
                bottom = {0: own} | {1 + j: up[begin + j] for j in range(last)}
                block = jnp.concatenate([chosen(top), chosen(bottom)], axis=0)
                env[one.joined] = block
        keys = list(fresh) + later.get(slot, [])
        for step in steps:
            keys += [name for name in step.needs if name in env and name not in keys]
        tied = [env[name] for name in keys]
        if sending:
            send_up, send_down, tied = lax.optimization_barrier((send_up, send_down, tied))
            up[slot] = lax.ppermute(send_up, "tp", [(p, p + 1) for p in up_options])
            down[slot] = lax.ppermute(send_down, "tp", [(p, p - 1) for p in down_options])
        elif tied:
            tied = lax.optimization_barrier(tied)
        env.update(zip(keys, tied))
        for one in sums:
            if slot == one.start + last:
                part = env[one.part]
                above = part[:half].astype(f32) + up[slot - 1].astype(f32)
                below = part[half:].astype(f32) + down[slot - 1].astype(f32)
                env[one.name + "_sum"] = jnp.where(place == last, above, below)
        fresh = []
        for step in steps:
            env.update(zip(step.gives, step.run(env)))
            if step.lasts:
                later.setdefault(step.until, []).extend(step.gives)
            else:
                fresh += [name for name in step.gives if name != awaited]
        ready = lax.optimization_barrier(tuple(mixed(o) for o in local_parts(slot + 1)))


def solution(mesh):
    in_specs = (
        P("seq", None),
        P("seq"),
        P(),
        P("seq", None, "tp"),
        P(None, "tp"),
        P("tp", "seq"),
        P(),
        P("seq", "tp"),
        P("seq", "tp"),
        P("tp", "seq"),
        P("seq", None),
    )
    out_specs = (
        P("seq", None),
        P("seq", None),
        P("seq", None, "tp"),
        P(None, "tp"),
        P("tp", "seq"),
        P("seq", "tp"),
        P("seq", "tp"),
        P("tp", "seq"),
        P(),
        P(),
    )
    return jax.shard_map(local, mesh=mesh, in_specs=in_specs, out_specs=out_specs, check_vma=False)
```

```python
import functools

import jax
import jax.numpy as jnp
from jax import lax
from jax.experimental import pallas as pl
from jax.experimental.pallas import tpu as pltpu
from jax.sharding import PartitionSpec as P

epsilon = 1e-05
bf16 = jnp.bfloat16
f32 = jnp.float32
halo = 16
chunks = 4


def dot_plain(left, right):
    return lax.dot_general(left, right, (((1,), (0,)), ((), ())), preferred_element_type=f32)


def dot_right(left, right):
    return lax.dot_general(left, right, (((1,), (1,)), ((), ())), preferred_element_type=f32)


def dot_left(left, right):
    return lax.dot_general(left, right, (((0,), (0,)), ((), ())), preferred_element_type=f32)


def rms_scale(value):
    return lax.rsqrt(jnp.mean(value * value, axis=1, keepdims=True) + epsilon)


def norm_back(grad_normed, scaled, inverse, gain):
    weighted = grad_normed * gain
    return inverse * (weighted - scaled * jnp.mean(weighted * scaled, axis=1, keepdims=True))


def from_before(block, axis):
    devices = lax.axis_size(axis)
    return lax.ppermute(block, axis, [(i, i + 1) for i in range(devices - 1)])


def from_after(block, axis):
    devices = lax.axis_size(axis)
    return lax.ppermute(block, axis, [(i + 1, i) for i in range(devices - 1)])


def bits_of(axis):
    devices = lax.axis_size(axis)
    return [1 << i for i in range(devices.bit_length() - 1)]


def paired(value, axis, bit):
    return lax.ppermute(value, axis, [(i, i ^ bit) for i in range(lax.axis_size(axis))])


def place_kernel(moves, here_ref, *refs):
    pieces, out, sems = refs[:-2], refs[-2], refs[-1]
    here = here_ref[0]
    copies = []
    for number, (piece, first, size, mask, offset, dim) in enumerate(moves):
        target = pl.ds(pl.multiple_of((here ^ mask) * size, size), size)
        other = pl.ds(offset, pieces[piece].shape[1 - dim])
        if dim == 0:
            source, place = pieces[piece].at[pl.ds(first, size), :], out.at[target, other]
        else:
            source, place = pieces[piece].at[:, pl.ds(first, size)], out.at[other, target]
        copies.append(pltpu.make_async_copy(source, place, sems.at[number]))
    for copy in copies:
        copy.start()
    for copy in copies:
        copy.wait()


def placed(pieces, shape, size, dim, here):
    moves = []
    for number, (_, masks, offset) in enumerate(pieces):
        moves += [(number, size * i, size, mask, offset, dim) for i, mask in enumerate(masks)]
    anywhere = pl.BlockSpec(memory_space=pl.ANY)
    return pl.pallas_call(
        functools.partial(place_kernel, moves),
        in_specs=[pl.BlockSpec(memory_space=pltpu.SMEM)] + [anywhere] * len(pieces),
        out_specs=pl.BlockSpec(memory_space=pltpu.VMEM),
        out_shape=jax.ShapeDtypeStruct(shape, bf16),
        scratch_shapes=[pltpu.SemaphoreType.DMA((len(moves),))],
        compiler_params=pltpu.CompilerParams(vmem_limit_bytes=2 * 2**20),
        cost_estimate=pl.CostEstimate(
            flops=0, bytes_accessed=4 * shape[0] * shape[1], transcendentals=0
        ),
    )(here.reshape(1), *[piece for piece, _, _ in pieces])


class Gather:
    def __init__(self, shards, axis):
        self.shards, self.axis = shards, axis
        self.devices = lax.axis_size(axis)
        self.outer = [1 << i for i in range(1, self.devices.bit_length() - 1)]
        self.plain = self.devices & (self.devices - 1) or len(self.outer) < 2
        self.turns = 0 if self.plain else len(self.outer) + 1
        self.turn, self.held, self.pieces, self.fresh = 0, {}, {}, []
        for number, (block, dim) in enumerate(shards):
            middle = block.shape[1 - dim] // 2
            for side in range(2):
                half = lax.slice_in_dim(block, side * middle, (side + 1) * middle, axis=1 - dim)
                self.held[number, side] = [(half, [0])]
            self.pieces[number] = [(block, [0], 0)]
            self.fresh.append((number, block, [0], 0))

    def sends(self):
        values = []
        self.bits, self.notes = [], []
        if self.turn < len(self.outer):
            for (number, side), parts in self.held.items():
                block, dim = self.shards[number]
                bit = (self.outer, self.outer[::-1])[side][self.turn]
                masks = [m ^ bit for _, ms in parts for m in ms]
                blocks = [part for part, _ in parts]
                values.append(jnp.concatenate(blocks, axis=dim) if self.turn else blocks[0])
                self.bits.append(bit)
                self.notes.append((number, side, masks, side * (block.shape[1 - dim] // 2)))
        for number, value, masks, offset in self.fresh:
            values.append(value)
            self.bits.append(1)
            self.notes.append((number, None, [m ^ 1 for m in masks], offset))
        return values

    def swap(self, values):
        got = []
        for value, bit in zip(values, self.bits):
            pairs = [(i, i ^ bit) for i in range(self.devices)]
            got.append(lax.ppermute(value, self.axis, pairs))
        return got

    def take(self, got):
        self.turn += 1
        self.fresh = []
        for value, (number, side, masks, offset) in zip(got, self.notes):
            self.pieces[number].append((value, masks, offset))
            if side is not None:
                self.held[number, side].append((value, masks))
                self.fresh.append((number, value, masks, offset))

    def whole(self):
        if self.plain:
            return [lax.all_gather(b, self.axis, axis=d, tiled=True) for b, d in self.shards]
        here = lax.axis_index(self.axis)
        results = []
        for number, (block, dim) in enumerate(self.shards):
            shape = list(block.shape)
            shape[dim] *= self.devices
            results.append(placed(self.pieces[number], shape, block.shape[dim], dim, here))
        return results


def together(gathers, run=None):
    live = [gather for gather in gathers if gather.turn < gather.turns]
    sends = lax.optimization_barrier([gather.sends() for gather in live])
    got = [gather.swap(values) for gather, values in zip(live, sends)]
    extra = run() if run else ()
    got, extra = lax.optimization_barrier((got, extra))
    for gather, values in zip(live, got):
        gather.take(values)
    return extra


def light(elements):
    return pl.CostEstimate(flops=elements, bytes_accessed=elements, transcendentals=0)


def feed_kernel(
    normed, grads, weights, act, grad_gate, grad_up, out, grad_normed, out_sum, grad_sum
):
    tile = pl.program_id(0)
    size = weights.shape[3]
    gate_w, up_w, down_w = (weights[:, i].reshape(-1, size) for i in range(3))
    gate = dot_plain(normed[...], gate_w)
    up = dot_plain(normed[...], up_w)
    grad_act = dot_plain(grads[...], down_w)
    sig = jax.nn.sigmoid(gate)
    swish = gate * sig
    act_here = (swish * up).astype(bf16)
    gate_here = (grad_act * up * sig * (1.0 + gate * (1.0 - sig))).astype(bf16)
    up_here = (grad_act * swish).astype(bf16)
    act[...] = act_here
    grad_gate[...] = gate_here
    grad_up[...] = up_here
    out_here = dot_right(act_here, down_w)
    grad_here = dot_right(gate_here, gate_w) + dot_right(up_here, up_w)

    @pl.when(tile == 0)
    def _():
        out_sum[...] = out_here
        grad_sum[...] = grad_here

    @pl.when(tile > 0)
    def _():
        out_sum[...] += out_here
        grad_sum[...] += grad_here

    @pl.when(tile == pl.num_programs(0) - 1)
    def _():
        out[...] = out_sum[...].astype(bf16)
        grad_normed[...] = grad_sum[...].astype(bf16)


def feed_forward(normed, grads, weights):
    rows, width = normed.shape
    devices, _, each, hidden = weights.shape
    tile = 512 if hidden % 512 == 0 else 256
    whole = pl.BlockSpec((rows, width), lambda j: (0, 0))
    block = pl.BlockSpec((devices, 3, each, tile), lambda j: (0, 0, 0, j))
    part = pl.BlockSpec((rows, tile), lambda j: (0, j))
    wide = jax.ShapeDtypeStruct((rows, hidden), bf16)
    narrow = jax.ShapeDtypeStruct((rows, width), bf16)
    return pl.pallas_call(
        feed_kernel,
        grid=(hidden // tile,),
        in_specs=[whole, whole, block],
        out_specs=[part, part, part, whole, whole],
        out_shape=[
            wide,
            wide,
            wide,
            narrow,
            narrow,
        ],
        scratch_shapes=[pltpu.VMEM((rows, width), f32)] * 2,
        compiler_params=pltpu.CompilerParams(vmem_limit_bytes=36 * 2**20),
        cost_estimate=pl.CostEstimate(
            flops=12 * rows * width * hidden,
            bytes_accessed=6 * width * hidden + 10 * rows * hidden,
            transcendentals=rows * hidden,
        ),
    )(normed, grads, weights)


def mixer_kernel(left, right, left_last, right_last, out):
    last = pl.num_programs(0) - 1

    @pl.when(pl.program_id(0) < last)
    def _():
        out[...] = dot_left(left[...], right[...]).astype(bf16)

    @pl.when(pl.program_id(0) == last)
    def _():
        out[...] = dot_left(left_last[...], right_last[...]).astype(bf16)


def mixer_products(left, right, left_last, right_last):
    count, width = left.shape
    tile = right_last.shape[1]
    tiles = right.shape[1] // tile
    whole = pl.BlockSpec((count, width), lambda j: (0, 0), pipeline_mode=pl.Buffered(1))
    return pl.pallas_call(
        mixer_kernel,
        grid=(tiles + 1,),
        in_specs=[
            whole,
            pl.BlockSpec((count, tile), lambda j: (0, jnp.minimum(j, tiles - 1))),
            whole,
            pl.BlockSpec((count, tile), lambda j: (0, 0)),
        ],
        out_specs=pl.BlockSpec((width, tile), lambda j: (0, j)),
        out_shape=jax.ShapeDtypeStruct((width, (tiles + 1) * tile), bf16),
        compiler_params=pltpu.CompilerParams(vmem_limit_bytes=24 * 2**20),
        cost_estimate=light(count * tile),
    )(left, right, left_last, right_last)


class Step:
    def __init__(self, name, needs, gives, run, cost, rank, lasts):
        self.name, self.needs, self.gives = name, needs, gives
        self.run, self.cost, self.rank, self.lasts = run, cost, rank, lasts
        self.alone = name.startswith(("small", "call"))


class Sum:
    def __init__(self, name, part, finish, own, joined, rank, back_rank):
        self.name, self.part, self.finish = name, part, finish
        self.own, self.joined, self.rank, self.back_rank = own, joined, rank, back_rank
        self.start = self.back = None


def plan(steps, sums, line, budget):
    slot_of = {}
    todo = list(steps)
    waiting = list(sums)
    finishing, returning, arriving = {}, [], {}
    slots = []
    slot = busy = 0
    while todo or waiting or returning or any(s >= slot for s in arriving):
        ready = [one for one in waiting if slot_of.get(one.part, slot) < slot]
        back = [one for one in returning if slot >= one.start + line]
        turn = [(one.rank, one) for one in ready] + [(one.back_rank, one) for one in back]
        if turn:
            one = min(turn, key=lambda t: t[0])[1]
            if one in ready:
                one.start = slot
                waiting.remove(one)
                returning.append(one)
                finishing.setdefault(slot + line - 1, []).append(one)
            else:
                one.back = slot
                returning.remove(one)
                arriving.setdefault(slot + line - 1, []).append(one)
        here = []
        spent = 0.0
        for one in finishing.get(slot, []):
            slot_of[one.name + "_sum"] = slot - 1
            step = next(s for s in todo if s.name == one.finish)
            here.append(step)
            todo.remove(step)
            spent += step.cost
            slot_of.update({name: slot for name in step.gives})
        for one in arriving.get(slot, []):
            slot_of[one.joined] = slot - 1
        again = True
        while again:
            again = False
            for step in sorted(todo, key=lambda s: s.rank):
                newest = max((slot_of.get(name, slot + 1) for name in step.needs), default=-1)
                ready = newest < slot if step.alone else newest <= slot
                if len(waiting) == len(sums):
                    fits = spent + step.cost <= 7.0
                elif step.rank[0] >= 5:
                    fits = spent <= 6.0 or spent + step.cost <= budget
                else:
                    fits = spent + step.cost <= budget or step.cost <= 3.0
                    fits = fits or (spent <= 4.0 and step.cost > budget)
                if ready and (spent == 0.0 or fits):
                    here.append(step)
                    todo.remove(step)
                    spent += step.cost
                    if step.lasts:
                        step.until = busy = max(busy, slot + 1) + step.lasts
                    until = step.until if step.lasts else slot
                    slot_of.update({name: until for name in step.gives})
                    again = True
                    break
        slots.append(here)
        slot += 1
    return slots


def local(
    tokens,
    doc_start,
    norm_first,
    in_weight,
    conv_weight,
    out_weight,
    norm_second,
    gate_weight,
    up_weight,
    down_weight,
    out_grad,
):
    line = lax.axis_size("tp")
    place = lax.axis_index("tp")
    count, width = tokens.shape
    rows = count // chunks
    half = rows // 2
    inner = conv_weight.shape[1]

    def tokens_of(c):
        return tokens[c * rows : (c + 1) * rows]

    def own_half(block):
        return jnp.where(place == line - 1, block[:half], block[half:])

    gain_one = norm_first.astype(f32)
    gain_two = norm_second.astype(f32)
    taps = conv_weight.astype(f32)
    kept_one = (1 - doc_start).astype(f32)[:, None]

    def normed(block):
        value = block.astype(f32)
        return (value * rms_scale(value) * gain_one).astype(bf16)

    before_tokens = from_before(tokens[count - halo :], "seq")
    before_kept = from_before(kept_one[count - 1 :], "seq")

    def norms():
        return normed(tokens), normed(before_tokens)

    def norms():
        return normed(tokens), normed(before_tokens)

    def held_back():
        return jnp.stack([gate_weight, up_weight, down_weight.T])

    in_full = lax.all_gather(
        in_weight.reshape(in_weight.shape[0], 3 * inner), "seq", axis=0, tiled=True
    )
    out_gather = Gather([(out_weight, 1)], "seq")
    feed_held = together([out_gather], held_back)
    normed_one, normed_before = together([out_gather], norms)
    while out_gather.turn < out_gather.turns:
        together([out_gather])
    (out_full,) = out_gather.whole()
    feed_full = lax.all_gather(feed_held, "seq")
    env = {}
    kept_back = jnp.concatenate([before_kept, kept_one[:-1]], axis=0)
    both_kept = kept_one * kept_back

    def kept_of(c):
        return kept_one[c * rows : (c + 1) * rows]

    def both_of(c):
        return both_kept[c * rows : (c + 1) * rows]

    steps = []
    sums = []

    def add(name, needs, gives, cost, rank, lasts=0):
        def keep(run):
            steps.append(Step(name, needs, gives, run, cost, rank, lasts))
            return run

        return keep

    def mix(c):
        def run_a(e):
            block = normed_one[c * rows : (c + 1) * rows]
            if c == 0:
                block = jnp.concatenate([normed_before, block], axis=0)
            projected = dot_plain(block, in_full).astype(bf16)
            left = projected[:, :inner].astype(f32)
            right = projected[:, 2 * inner :].astype(f32)
            product = left * right
            if c == 0:
                earlier = product[halo - 2 : halo]
                product = product[halo:]
                projected = projected[halo:]
            else:
                earlier = e[f"tail{c - 1}"]
            longer = jnp.concatenate([earlier, product], axis=0)
            convolved = (
                taps[0] * product
                + taps[1] * kept_of(c) * longer[1:-1]
                + taps[2] * both_of(c) * longer[:-2]
            )
            gated = (projected[:, inner : 2 * inner].astype(f32) * convolved).astype(bf16)
            return projected, longer, product[-2:], convolved, gated

        def run_b(e):
            return (dot_plain(e[f"gated{c}"], out_full).astype(bf16),)

        gives = [f"{n}{c}" for n in ("proj", "longer", "tail", "conv", "gated")]
        needs = [] if c == 0 else [f"tail{c - 1}"]
        add(f"mixA{c}", needs, gives, 5.0, (0, c))(run_a)
        add(f"mixB{c}", [f"gated{c}"], [f"mixed{c}"], 2.0, (0, c))(run_b)

    def first(c):
        def run(e):
            hidden = own_half(tokens_of(c)).astype(f32) + e[f"one{c}_sum"]
            inverse = rms_scale(hidden)
            return hidden, inverse, (hidden * inverse * gain_two).astype(bf16)

        add(f"first{c}", [f"one{c}_sum"], [f"hid{c}", f"inv{c}", f"n2own{c}"], 2.0, (1, c))(run)
        sums.append(Sum(f"one{c}", f"mixed{c}", f"first{c}", f"n2own{c}", f"n2{c}", (0, c), (0.5, c)))

    def feed(c):
        def run(e):
            grads = out_grad[c * rows : (c + 1) * rows]
            return feed_forward(e[f"n2{c}"], grads, feed_full)

        gives = [f"act{c}", f"gg{c}", f"gu{c}", f"fo{c}", f"gn2{c}"]
        add(f"feed{c}", [f"n2{c}"], gives, 22.0, (2, c))(run)

    def second(c):
        def run(e):
            hidden, inverse = e[f"hid{c}"], e[f"inv{c}"]
            scaled = hidden * inverse
            grad_normed = e[f"two{c}_sum"]
            grad_hidden = own_half(out_grad[c * rows : (c + 1) * rows]).astype(f32) + norm_back(
                grad_normed, scaled, inverse, gain_two
            )
            return grad_hidden, grad_hidden.astype(bf16), jnp.sum(grad_normed * scaled, axis=0)

        gives = [f"gh{c}", f"gmown{c}", f"g2{c}"]
        add(f"second{c}", [f"two{c}_sum", f"hid{c}", f"inv{c}"], gives, 3.0, (1, c))(run)
        sums.append(Sum(f"two{c}", f"gn2{c}", f"second{c}", f"gmown{c}", f"gm{c}", (1, c), (1.5, c)))

    def third(last):
        def run_part(e):
            blocks = []
            for c in range(last):
                part = e[f"fo{c}"].astype(f32)
                top = jnp.where(place == line - 1, e[f"hid{c}"], 0.0)
                bottom = jnp.where(place == 0, e[f"hid{c}"], 0.0)
                blocks += [part[:half] + top, part[half:] + bottom]
            return (lax.psum(jnp.concatenate(blocks, axis=0).astype(bf16), "tp"),)

        needs = [f"{n}{c}" for n in ("fo", "hid") for c in range(last)]
        add("third0", needs, ["out0"], 3.0, (2.5, 0), 4)(run_part)

    def third_line(c):
        def run(e):
            return ((e[f"hid{c}"] + e[f"three{c}_sum"]).astype(bf16),)

        add(f"third{c}", [f"three{c}_sum", f"hid{c}"], [f"outown{c}"], 1.0, (1, c))(run)
        sums.append(Sum(f"three{c}", f"fo{c}", f"third{c}", f"outown{c}", f"out{c}", (3, c), (5, c)))

    def back(c):
        def run_a(e):
            grad_gated = dot_right(e[f"gm{c}"], out_full).astype(bf16).astype(f32)
            grad_conv = grad_gated * e[f"proj{c}"][:, inner : 2 * inner].astype(f32)
            grad_out = (grad_gated * e[f"conv{c}"]).astype(bf16)
            longer = e[f"longer{c}"]
            near = grad_conv * kept_of(c)
            far = grad_conv * both_of(c)
            tap_sums = jnp.stack(
                [
                    jnp.sum(grad_conv * longer[2:], axis=0),
                    jnp.sum(near * longer[1:-1], axis=0),
                    jnp.sum(far * longer[:-2], axis=0),
                ]
            )
            head = jnp.concatenate([near[:1], far[:2]], axis=0)
            passed = (from_after(head, "seq"),) if c == 0 else ()
            return (grad_conv, grad_out, tap_sums, head) + passed

        def run_b(e):
            grad_conv = e[f"gc{c}"]
            head = e[f"head{c + 1}"]
            near = jnp.concatenate([(grad_conv * kept_of(c))[1:], head[:1]], axis=0)
            far = jnp.concatenate([(grad_conv * both_of(c))[2:], head[1:]], axis=0)
            grad_product = taps[0] * grad_conv + taps[1] * near + taps[2] * far
            left = e[f"proj{c}"][:, :inner].astype(f32)
            right = e[f"proj{c}"][:, 2 * inner :].astype(f32)
            grad_projected = jnp.concatenate(
                [
                    (grad_product * right).astype(bf16),
                    e[f"go{c}"],
                    (grad_product * left).astype(bf16),
                ],
                axis=1,
            )
            grad_normed = dot_right(grad_projected, in_full).astype(bf16)
            value = tokens_of(c).astype(f32)
            gain_sum = jnp.sum(grad_normed.astype(f32) * (value * rms_scale(value)), axis=0)
            return grad_projected, grad_normed, gain_sum

        needs = [f"gm{c}", f"proj{c}", f"longer{c}", f"conv{c}"]
        gives = [f"gc{c}", f"go{c}", f"tap{c}", f"head{c}"]
        gives += [f"head{chunks}"] if c == 0 else []
        add(f"backA{c}", needs, gives, 5.0, (2, c))(run_a)
        needs = [f"gc{c}", f"go{c}", f"proj{c}", f"head{c + 1}"]
        add(f"backB{c}", needs, [f"gp{c}", f"gn1{c}", f"g1{c}"], 9.0, (3, c))(run_b)

    def fourth(c):
        def run(e):
            value = own_half(tokens_of(c)).astype(f32)
            inverse = rms_scale(value)
            scaled = value * inverse
            grad_normed = e[f"four{c}_sum"]
            grad_tokens = e[f"gh{c}"] + norm_back(grad_normed, scaled, inverse, gain_one)
            return (grad_tokens.astype(bf16),)

        add(f"fourth{c}", [f"four{c}_sum", f"gh{c}"], [f"gtown{c}"], 3.0, (1, c))(run)
        sums.append(Sum(f"four{c}", f"gn1{c}", f"fourth{c}", f"gtown{c}", f"gt{c}", (2, c), (4, c)))

    for c in range(chunks):
        mix(c)
    for c in range(chunks):
        first(c)
        feed(c)
        second(c)
        back(c)
        fourth(c)

    third(chunks // 2)
    for c in range(chunks // 2, chunks):
        third_line(c)

    def joined(e, name):
        return jnp.concatenate([e[f"{name}{c}"] for c in range(chunks)], axis=0)

    def names(*kinds):
        return [f"{kind}{c}" for kind in kinds for c in range(chunks)]

    def scattered_sum(name, needs, run, cost, order, dim, lasts):
        add(f"{name}_part", needs, [f"{name}_part"], cost, (5, order))(run)

        def call(e):
            return (lax.psum_scatter(e[f"{name}_part"], "seq", scatter_dimension=dim, tiled=True),)

        add(f"call_{name}", [f"{name}_part"], [name], 0.0, (2.6, 9 + order), lasts)(call)

    def down_part(e):
        return (dot_left(joined(e, "act"), out_grad).astype(bf16),)

    def gate_part(e):
        return (dot_left(joined(e, "n2"), joined(e, "gg")).astype(bf16),)

    def up_part(e):
        return (dot_left(joined(e, "n2"), joined(e, "gu")).astype(bf16),)

    def mixer_part(e):
        return (mixer_products(normed_one, joined(e, "gp"), joined(e, "gm"), joined(e, "gated")),)

    scattered_sum("down_grad", names("act"), down_part, 12.0, 0, 1, 3)
    scattered_sum("gate_grad", names("n2", "gg"), gate_part, 11.0, 1, 0, 4)
    scattered_sum("up_grad", names("n2", "gu"), up_part, 11.0, 1.5, 0, 4)
    scattered_sum("mixer_grad", names("gm", "gated", "gp"), mixer_part, 18.0, 2, 0, 4)

    def total(e, kind):
        return sum(e[f"{kind}{c}"] for c in range(chunks))

    def small(e):
        owner = (place == 0) | (place == line - 1)
        gains = jnp.stack([total(e, "g1"), jnp.where(owner, total(e, "g2"), 0.0)])
        return (jnp.concatenate([gains.reshape(-1, inner), total(e, "tap")], axis=0),)

    add("small", names("g1", "g2", "tap"), ["small0"], 2.0, (4, 9))(small)
    turn = 0
    for axis in ("seq", "tp"):
        for bit in bits_of(axis):

            def run(e, axis=axis, bit=bit, turn=turn):
                value = e[f"small{turn}"]
                if axis == "seq":
                    return (value + paired(value, axis, bit),)
                gains = value[:-3] + paired(value[:-3], axis, bit)
                return (jnp.concatenate([gains, value[-3:]], axis=0),)

            add(f"small{turn + 1}", [f"small{turn}"], [f"small{turn + 1}"], 2.0, (4, 10))(run)
            turn += 1

    def rows_put(name, needs, first, step):
        def run(e):
            block = e[needs[0]].astype(f32 if name == "tokens_grad" else bf16)
            if len(needs) == 1:
                return (jnp.pad(block, ((0, count - block.shape[0]), (0, 0))),)
            return (lax.dynamic_update_slice(e[needs[1]], block, (first, 0)),)

        add(f"{name}_{step}", needs, [f"{name}{step}"], 2.0, (4.6, step))(run)

    for c in range(chunks):
        so_far = [f"tokens_grad{c - 1}"] if c else []
        rows_put("tokens_grad", [f"gt{c}"] + so_far, c * rows, c)
    rows_put("block_out", ["out0"], 0, 0)
    for c in range(chunks // 2, chunks):
        step = c - chunks // 2 + 1
        rows_put("block_out", [f"out{c}", f"block_out{step - 1}"], c * rows, step)

    def widened(name):
        add(f"{name}_wide", [f"{name}_grad"], [f"{name}_wide"], 2.0, (4.7, 0))(
            lambda e: (e[f"{name}_grad"].astype(f32),)
        )

    for name in ("down", "gate", "up"):
        widened(name)

    def mixer_wide(e):
        mixer_grad = e["mixer_grad"].astype(f32)
        return mixer_grad[:, : 3 * inner].reshape(in_weight.shape), mixer_grad[:, 3 * inner :].T

    add("mixer_wide", ["mixer_grad"], ["in_wide", "out_wide"], 3.0, (4.5, 1))(mixer_wide)

    slots = plan(steps, sums, line, 16.0)
    run_slots(slots, sums, env, line, place, half)

    gains = env[f"small{turn}"][:-3].reshape(2, width)
    return (
        env[f"block_out{chunks - chunks // 2}"],
        env[f"tokens_grad{chunks - 1}"],
        env["in_wide"],
        env[f"small{turn}"][-3:],
        env["out_wide"],
        env["gate_wide"],
        env["up_wide"],
        env["down_wide"],
        gains[0],
        gains[1],
    )


def run_slots(slots, sums, env, line, place, half):
    up, down = {}, {}
    last = line - 1
    fresh, later = [], {}
    awaited = f"head{chunks}"

    def chosen(options):
        value = None
        for position, option in sorted(options.items(), reverse=True):
            if value is None or option is value:
                value = option
            else:
                value = jnp.where(place == position, option, value)
        return value

    def local_parts(slot):
        up_options, down_options = {}, {}
        for one in sums:
            hop = slot - one.start
            if 0 <= hop < last:
                part = env[one.part]
                up_options[hop] = part[:half]
                down_options[last - hop] = part[half:]
            hop = slot - one.back
            if 0 <= hop < last:
                value = env[one.own] if hop == 0 else None
                up_options[hop] = down_options[last - hop] = value
        return up_options, down_options

    def mixed(options):
        if all(value is None for value in options.values()):
            return None
        return chosen({p: 0.0 if value is None else value for p, value in options.items()})

    ready = None
    for slot, steps in enumerate(slots):
        up_options, down_options = local_parts(slot)
        sending = len(up_options) > 0
        if sending:
            send_up, send_down = ready if ready is not None else (None, None)
            if ready is None:
                send_up, send_down = mixed(up_options), mixed(down_options)
            if slot - 1 in up:
                send_up = up[slot - 1] if send_up is None else send_up + up[slot - 1]
                send_down = down[slot - 1] if send_down is None else send_down + down[slot - 1]
        for one in sums:
            if slot == one.back + last:
                own, begin = env[one.own], one.back
                top = {last: own} | {last - 1 - j: down[begin + j] for j in range(last)}
                bottom = {0: own} | {1 + j: up[begin + j] for j in range(last)}
                block = jnp.concatenate([chosen(top), chosen(bottom)], axis=0)
                env[one.joined] = block
        keys = list(fresh) + later.get(slot, [])
        for step in steps:
            keys += [name for name in step.needs if name in env and name not in keys]
        tied = [env[name] for name in keys]
        if sending:
            send_up, send_down, tied = lax.optimization_barrier((send_up, send_down, tied))
            up[slot] = lax.ppermute(send_up, "tp", [(p, p + 1) for p in up_options])
            down[slot] = lax.ppermute(send_down, "tp", [(p, p - 1) for p in down_options])
        elif tied:
            tied = lax.optimization_barrier(tied)
        env.update(zip(keys, tied))
        for one in sums:
            if slot == one.start + last:
                part = env[one.part]
                above = part[:half].astype(f32) + up[slot - 1].astype(f32)
                below = part[half:].astype(f32) + down[slot - 1].astype(f32)
                env[one.name + "_sum"] = jnp.where(place == last, above, below)
        fresh = []
        for step in steps:
            env.update(zip(step.gives, step.run(env)))
            if step.lasts:
                later.setdefault(step.until, []).extend(step.gives)
            else:
                fresh += [name for name in step.gives if name != awaited]
        ready = lax.optimization_barrier(tuple(mixed(o) for o in local_parts(slot + 1)))


def solution(mesh):
    in_specs = (
        P("seq", None),
        P("seq"),
        P(),
        P("seq", None, "tp"),
        P(None, "tp"),
        P("tp", "seq"),
        P(),
        P("seq", "tp"),
        P("seq", "tp"),
        P("tp", "seq"),
        P("seq", None),
    )
    out_specs = (
        P("seq", None),
        P("seq", None),
        P("seq", None, "tp"),
        P(None, "tp"),
        P("tp", "seq"),
        P("seq", "tp"),
        P("seq", "tp"),
        P("tp", "seq"),
        P(),
        P(),
    )
    return jax.shard_map(local, mesh=mesh, in_specs=in_specs, out_specs=out_specs, check_vma=False)
```

```python
import functools

import jax
import jax.numpy as jnp
from jax import lax
from jax.experimental import pallas as pl
from jax.experimental.pallas import tpu as pltpu
from jax.sharding import PartitionSpec as P

epsilon = 1e-05
bf16 = jnp.bfloat16
f32 = jnp.float32
halo = 16
chunks = 4


def dot_plain(left, right):
    return lax.dot_general(left, right, (((1,), (0,)), ((), ())), preferred_element_type=f32)


def dot_right(left, right):
    return lax.dot_general(left, right, (((1,), (1,)), ((), ())), preferred_element_type=f32)


def dot_left(left, right):
    return lax.dot_general(left, right, (((0,), (0,)), ((), ())), preferred_element_type=f32)


def rms_scale(value):
    return lax.rsqrt(jnp.mean(value * value, axis=1, keepdims=True) + epsilon)


def norm_back(grad_normed, scaled, inverse, gain):
    weighted = grad_normed * gain
    return inverse * (weighted - scaled * jnp.mean(weighted * scaled, axis=1, keepdims=True))


def from_before(block, axis):
    devices = lax.axis_size(axis)
    return lax.ppermute(block, axis, [(i, i + 1) for i in range(devices - 1)])


def from_after(block, axis):
    devices = lax.axis_size(axis)
    return lax.ppermute(block, axis, [(i + 1, i) for i in range(devices - 1)])


def bits_of(axis):
    devices = lax.axis_size(axis)
    return [1 << i for i in range(devices.bit_length() - 1)]


def paired(value, axis, bit):
    return lax.ppermute(value, axis, [(i, i ^ bit) for i in range(lax.axis_size(axis))])


def place_kernel(moves, here_ref, *refs):
    pieces, out, sems = refs[:-2], refs[-2], refs[-1]
    here = here_ref[0]
    copies = []
    for number, (piece, first, size, mask, offset, dim) in enumerate(moves):
        target = pl.ds(pl.multiple_of((here ^ mask) * size, size), size)
        other = pl.ds(offset, pieces[piece].shape[1 - dim])
        if dim == 0:
            source, place = pieces[piece].at[pl.ds(first, size), :], out.at[target, other]
        else:
            source, place = pieces[piece].at[:, pl.ds(first, size)], out.at[other, target]
        copies.append(pltpu.make_async_copy(source, place, sems.at[number]))
    for copy in copies:
        copy.start()
    for copy in copies:
        copy.wait()


def placed(pieces, shape, size, dim, here):
    moves = []
    for number, (_, masks, offset) in enumerate(pieces):
        moves += [(number, size * i, size, mask, offset, dim) for i, mask in enumerate(masks)]
    anywhere = pl.BlockSpec(memory_space=pl.ANY)
    return pl.pallas_call(
        functools.partial(place_kernel, moves),
        in_specs=[pl.BlockSpec(memory_space=pltpu.SMEM)] + [anywhere] * len(pieces),
        out_specs=pl.BlockSpec(memory_space=pltpu.VMEM),
        out_shape=jax.ShapeDtypeStruct(shape, bf16),
        scratch_shapes=[pltpu.SemaphoreType.DMA((len(moves),))],
        compiler_params=pltpu.CompilerParams(vmem_limit_bytes=2 * 2**20),
        cost_estimate=pl.CostEstimate(
            flops=0, bytes_accessed=4 * shape[0] * shape[1], transcendentals=0
        ),
    )(here.reshape(1), *[piece for piece, _, _ in pieces])


class Gather:
    def __init__(self, shards, axis):
        self.shards, self.axis = shards, axis
        self.devices = lax.axis_size(axis)
        self.outer = [1 << i for i in range(1, self.devices.bit_length() - 1)]
        self.plain = self.devices & (self.devices - 1) or len(self.outer) < 2
        self.turns = 0 if self.plain else len(self.outer) + 1
        self.turn, self.held, self.pieces, self.fresh = 0, {}, {}, []
        for number, (block, dim) in enumerate(shards):
            middle = block.shape[1 - dim] // 2
            for side in range(2):
                half = lax.slice_in_dim(block, side * middle, (side + 1) * middle, axis=1 - dim)
                self.held[number, side] = [(half, [0])]
            self.pieces[number] = [(block, [0], 0)]
            self.fresh.append((number, block, [0], 0))

    def sends(self):
        values = []
        self.bits, self.notes = [], []
        if self.turn < len(self.outer):
            for (number, side), parts in self.held.items():
                block, dim = self.shards[number]
                bit = (self.outer, self.outer[::-1])[side][self.turn]
                masks = [m ^ bit for _, ms in parts for m in ms]
                blocks = [part for part, _ in parts]
                values.append(jnp.concatenate(blocks, axis=dim) if self.turn else blocks[0])
                self.bits.append(bit)
                self.notes.append((number, side, masks, side * (block.shape[1 - dim] // 2)))
        for number, value, masks, offset in self.fresh:
            values.append(value)
            self.bits.append(1)
            self.notes.append((number, None, [m ^ 1 for m in masks], offset))
        return values

    def swap(self, values):
        got = []
        for value, bit in zip(values, self.bits):
            pairs = [(i, i ^ bit) for i in range(self.devices)]
            got.append(lax.ppermute(value, self.axis, pairs))
        return got

    def take(self, got):
        self.turn += 1
        self.fresh = []
        for value, (number, side, masks, offset) in zip(got, self.notes):
            self.pieces[number].append((value, masks, offset))
            if side is not None:
                self.held[number, side].append((value, masks))
                self.fresh.append((number, value, masks, offset))

    def whole(self):
        if self.plain:
            return [lax.all_gather(b, self.axis, axis=d, tiled=True) for b, d in self.shards]
        here = lax.axis_index(self.axis)
        results = []
        for number, (block, dim) in enumerate(self.shards):
            shape = list(block.shape)
            shape[dim] *= self.devices
            results.append(placed(self.pieces[number], shape, block.shape[dim], dim, here))
        return results


def together(gathers, run=None):
    live = [gather for gather in gathers if gather.turn < gather.turns]
    sends = lax.optimization_barrier([gather.sends() for gather in live])
    got = [gather.swap(values) for gather, values in zip(live, sends)]
    extra = run() if run else ()
    got, extra = lax.optimization_barrier((got, extra))
    for gather, values in zip(live, got):
        gather.take(values)
    return extra


def light(elements):
    return pl.CostEstimate(flops=elements, bytes_accessed=elements, transcendentals=0)


def feed_kernel(
    normed, grads, weights, act, grad_gate, grad_up, out, grad_normed, out_sum, grad_sum
):
    tile = pl.program_id(0)
    size = weights.shape[3]
    gate_w, up_w, down_w = (weights[:, i].reshape(-1, size) for i in range(3))
    gate = dot_plain(normed[...], gate_w)
    up = dot_plain(normed[...], up_w)
    grad_act = dot_plain(grads[...], down_w)
    sig = jax.nn.sigmoid(gate)
    swish = gate * sig
    act_here = (swish * up).astype(bf16)
    gate_here = (grad_act * up * sig * (1.0 + gate * (1.0 - sig))).astype(bf16)
    up_here = (grad_act * swish).astype(bf16)
    act[...] = act_here
    grad_gate[...] = gate_here
    grad_up[...] = up_here
    out_here = dot_right(act_here, down_w)
    grad_here = dot_right(gate_here, gate_w) + dot_right(up_here, up_w)

    @pl.when(tile == 0)
    def _():
        out_sum[...] = out_here
        grad_sum[...] = grad_here

    @pl.when(tile > 0)
    def _():
        out_sum[...] += out_here
        grad_sum[...] += grad_here

    @pl.when(tile == pl.num_programs(0) - 1)
    def _():
        out[...] = out_sum[...].astype(bf16)
        grad_normed[...] = grad_sum[...].astype(bf16)


def feed_forward(normed, grads, weights):
    rows, width = normed.shape
    devices, _, each, hidden = weights.shape
    tile = 512 if hidden % 512 == 0 else 256
    whole = pl.BlockSpec((rows, width), lambda j: (0, 0))
    block = pl.BlockSpec((devices, 3, each, tile), lambda j: (0, 0, 0, j))
    part = pl.BlockSpec((rows, tile), lambda j: (0, j))
    wide = jax.ShapeDtypeStruct((rows, hidden), bf16)
    narrow = jax.ShapeDtypeStruct((rows, width), bf16)
    return pl.pallas_call(
        feed_kernel,
        grid=(hidden // tile,),
        in_specs=[whole, whole, block],
        out_specs=[part, part, part, whole, whole],
        out_shape=[
            wide,
            wide,
            wide,
            narrow,
            narrow,
        ],
        scratch_shapes=[pltpu.VMEM((rows, width), f32)] * 2,
        compiler_params=pltpu.CompilerParams(vmem_limit_bytes=36 * 2**20),
        cost_estimate=pl.CostEstimate(
            flops=12 * rows * width * hidden,
            bytes_accessed=6 * width * hidden + 10 * rows * hidden,
            transcendentals=rows * hidden,
        ),
    )(normed, grads, weights)


def mixer_kernel(left, right, left_last, right_last, out):
    last = pl.num_programs(0) - 1

    @pl.when(pl.program_id(0) < last)
    def _():
        out[...] = dot_left(left[...], right[...]).astype(bf16)

    @pl.when(pl.program_id(0) == last)
    def _():
        out[...] = dot_left(left_last[...], right_last[...]).astype(bf16)


def mixer_products(left, right, left_last, right_last):
    count, width = left.shape
    tile = right_last.shape[1]
    tiles = right.shape[1] // tile
    whole = pl.BlockSpec((count, width), lambda j: (0, 0), pipeline_mode=pl.Buffered(1))
    return pl.pallas_call(
        mixer_kernel,
        grid=(tiles + 1,),
        in_specs=[
            whole,
            pl.BlockSpec((count, tile), lambda j: (0, jnp.minimum(j, tiles - 1))),
            whole,
            pl.BlockSpec((count, tile), lambda j: (0, 0)),
        ],
        out_specs=pl.BlockSpec((width, tile), lambda j: (0, j)),
        out_shape=jax.ShapeDtypeStruct((width, (tiles + 1) * tile), bf16),
        compiler_params=pltpu.CompilerParams(vmem_limit_bytes=24 * 2**20),
        cost_estimate=light(count * tile),
    )(left, right, left_last, right_last)


class Step:
    def __init__(self, name, needs, gives, run, cost, rank, lasts):
        self.name, self.needs, self.gives = name, needs, gives
        self.run, self.cost, self.rank, self.lasts = run, cost, rank, lasts
        self.alone = name.startswith(("small", "call"))


class Sum:
    def __init__(self, name, part, finish, own, joined, rank, back_rank):
        self.name, self.part, self.finish = name, part, finish
        self.own, self.joined, self.rank, self.back_rank = own, joined, rank, back_rank
        self.start = self.back = None


def plan(steps, sums, line, budget):
    slot_of = {}
    todo = list(steps)
    waiting = list(sums)
    finishing, returning, arriving = {}, [], {}
    slots = []
    slot = busy = 0
    while todo or waiting or returning or any(s >= slot for s in arriving):
        ready = [one for one in waiting if slot_of.get(one.part, slot) < slot]
        back = [one for one in returning if slot >= one.start + line]
        turn = [(one.rank, one) for one in ready] + [(one.back_rank, one) for one in back]
        if turn:
            one = min(turn, key=lambda t: t[0])[1]
            if one in ready:
                one.start = slot
                waiting.remove(one)
                returning.append(one)
                finishing.setdefault(slot + line - 1, []).append(one)
            else:
                one.back = slot
                returning.remove(one)
                arriving.setdefault(slot + line - 1, []).append(one)
        here = []
        spent = 0.0
        for one in finishing.get(slot, []):
            slot_of[one.name + "_sum"] = slot - 1
            step = next(s for s in todo if s.name == one.finish)
            here.append(step)
            todo.remove(step)
            spent += step.cost
            slot_of.update({name: slot for name in step.gives})
        for one in arriving.get(slot, []):
            slot_of[one.joined] = slot - 1
        again = True
        while again:
            again = False
            for step in sorted(todo, key=lambda s: s.rank):
                newest = max((slot_of.get(name, slot + 1) for name in step.needs), default=-1)
                ready = newest < slot if step.alone else newest <= slot
                if len(waiting) == len(sums):
                    fits = spent + step.cost <= 7.0
                elif step.rank[0] >= 5:
                    fits = spent <= 6.0 or spent + step.cost <= budget
                else:
                    fits = spent + step.cost <= budget or step.cost <= 3.0
                    fits = fits or (spent <= 4.0 and step.cost > budget)
                if ready and (spent == 0.0 or fits):
                    here.append(step)
                    todo.remove(step)
                    spent += step.cost
                    if step.lasts:
                        step.until = busy = max(busy, slot + 1) + step.lasts
                    until = step.until if step.lasts else slot
                    slot_of.update({name: until for name in step.gives})
                    again = True
                    break
        slots.append(here)
        slot += 1
    return slots


def local(
    tokens,
    doc_start,
    norm_first,
    in_weight,
    conv_weight,
    out_weight,
    norm_second,
    gate_weight,
    up_weight,
    down_weight,
    out_grad,
):
    line = lax.axis_size("tp")
    place = lax.axis_index("tp")
    count, width = tokens.shape
    rows = count // chunks
    half = rows // 2
    inner = conv_weight.shape[1]

    def tokens_of(c):
        return tokens[c * rows : (c + 1) * rows]

    def own_half(block):
        return jnp.where(place == line - 1, block[:half], block[half:])

    gain_one = norm_first.astype(f32)
    gain_two = norm_second.astype(f32)
    taps = conv_weight.astype(f32)
    kept_one = (1 - doc_start).astype(f32)[:, None]

    def normed(block):
        value = block.astype(f32)
        return (value * rms_scale(value) * gain_one).astype(bf16)

    before_tokens = from_before(tokens[count - halo :], "seq")
    before_kept = from_before(kept_one[count - 1 :], "seq")

    def norms():
        return normed(tokens), normed(before_tokens)

    def norms():
        return normed(tokens), normed(before_tokens)

    def held_back():
        return jnp.stack([gate_weight, up_weight, down_weight.T])

    in_full = lax.all_gather(
        in_weight.reshape(in_weight.shape[0], 3 * inner), "seq", axis=0, tiled=True
    )
    out_gather = Gather([(out_weight, 1)], "seq")
    feed_held = together([out_gather], held_back)
    normed_one, normed_before = together([out_gather], norms)
    while out_gather.turn < out_gather.turns:
        together([out_gather])
    (out_full,) = out_gather.whole()
    feed_full = lax.all_gather(feed_held, "seq")
    env = {}
    kept_back = jnp.concatenate([before_kept, kept_one[:-1]], axis=0)
    both_kept = kept_one * kept_back

    def kept_of(c):
        return kept_one[c * rows : (c + 1) * rows]

    def both_of(c):
        return both_kept[c * rows : (c + 1) * rows]

    steps = []
    sums = []

    def add(name, needs, gives, cost, rank, lasts=0):
        def keep(run):
            steps.append(Step(name, needs, gives, run, cost, rank, lasts))
            return run

        return keep

    def mix(c):
        def run_a(e):
            block = normed_one[c * rows : (c + 1) * rows]
            if c == 0:
                block = jnp.concatenate([normed_before, block], axis=0)
            projected = dot_plain(block, in_full).astype(bf16)
            left = projected[:, :inner].astype(f32)
            right = projected[:, 2 * inner :].astype(f32)
            product = left * right
            if c == 0:
                earlier = product[halo - 2 : halo]
                product = product[halo:]
                projected = projected[halo:]
            else:
                earlier = e[f"tail{c - 1}"]
            longer = jnp.concatenate([earlier, product], axis=0)
            convolved = (
                taps[0] * product
                + taps[1] * kept_of(c) * longer[1:-1]
                + taps[2] * both_of(c) * longer[:-2]
            )
            gated = (projected[:, inner : 2 * inner].astype(f32) * convolved).astype(bf16)
            return projected, longer, product[-2:], convolved, gated

        def run_b(e):
            return (dot_plain(e[f"gated{c}"], out_full).astype(bf16),)

        gives = [f"{n}{c}" for n in ("proj", "longer", "tail", "conv", "gated")]
        needs = [] if c == 0 else [f"tail{c - 1}"]
        add(f"mixA{c}", needs, gives, 5.0, (0, c))(run_a)
        add(f"mixB{c}", [f"gated{c}"], [f"mixed{c}"], 2.0, (0, c))(run_b)

    def first(c):
        def run(e):
            hidden = own_half(tokens_of(c)).astype(f32) + e[f"one{c}_sum"]
            inverse = rms_scale(hidden)
            return hidden, inverse, (hidden * inverse * gain_two).astype(bf16)

        add(f"first{c}", [f"one{c}_sum"], [f"hid{c}", f"inv{c}", f"n2own{c}"], 2.0, (1, c))(run)
        sums.append(Sum(f"one{c}", f"mixed{c}", f"first{c}", f"n2own{c}", f"n2{c}", (0, c), (0.5, c)))

    def feed(c):
        def run(e):
            grads = out_grad[c * rows : (c + 1) * rows]
            return feed_forward(e[f"n2{c}"], grads, feed_full)

        gives = [f"act{c}", f"gg{c}", f"gu{c}", f"fo{c}", f"gn2{c}"]
        add(f"feed{c}", [f"n2{c}"], gives, 22.0, (2, c))(run)

    def second(c):
        def run(e):
            hidden, inverse = e[f"hid{c}"], e[f"inv{c}"]
            scaled = hidden * inverse
            grad_normed = e[f"two{c}_sum"]
            grad_hidden = own_half(out_grad[c * rows : (c + 1) * rows]).astype(f32) + norm_back(
                grad_normed, scaled, inverse, gain_two
            )
            return grad_hidden, grad_hidden.astype(bf16), jnp.sum(grad_normed * scaled, axis=0)

        gives = [f"gh{c}", f"gmown{c}", f"g2{c}"]
        add(f"second{c}", [f"two{c}_sum", f"hid{c}", f"inv{c}"], gives, 3.0, (1, c))(run)
        sums.append(Sum(f"two{c}", f"gn2{c}", f"second{c}", f"gmown{c}", f"gm{c}", (1, c), (1.5, c)))

    def third(last):
        def run_part(e):
            blocks = []
            for c in range(last):
                part = e[f"fo{c}"].astype(f32)
                top = jnp.where(place == line - 1, e[f"hid{c}"], 0.0)
                bottom = jnp.where(place == 0, e[f"hid{c}"], 0.0)
                blocks += [part[:half] + top, part[half:] + bottom]
            return (lax.psum(jnp.concatenate(blocks, axis=0).astype(bf16), "tp"),)

        needs = [f"{n}{c}" for n in ("fo", "hid") for c in range(last)]
        add("third0", needs, ["out0"], 3.0, (2.5, 0), 5)(run_part)

    def third_line(c):
        def run(e):
            return ((e[f"hid{c}"] + e[f"three{c}_sum"]).astype(bf16),)

        add(f"third{c}", [f"three{c}_sum", f"hid{c}"], [f"outown{c}"], 1.0, (1, c))(run)
        sums.append(Sum(f"three{c}", f"fo{c}", f"third{c}", f"outown{c}", f"out{c}", (3, c), (5, c)))

    def back(c):
        def run_a(e):
            grad_gated = dot_right(e[f"gm{c}"], out_full).astype(bf16).astype(f32)
            grad_conv = grad_gated * e[f"proj{c}"][:, inner : 2 * inner].astype(f32)
            grad_out = (grad_gated * e[f"conv{c}"]).astype(bf16)
            longer = e[f"longer{c}"]
            near = grad_conv * kept_of(c)
            far = grad_conv * both_of(c)
            tap_sums = jnp.stack(
                [
                    jnp.sum(grad_conv * longer[2:], axis=0),
                    jnp.sum(near * longer[1:-1], axis=0),
                    jnp.sum(far * longer[:-2], axis=0),
                ]
            )
            head = jnp.concatenate([near[:1], far[:2]], axis=0)
            passed = (from_after(head, "seq"),) if c == 0 else ()
            return (grad_conv, grad_out, tap_sums, head) + passed

        def run_b(e):
            grad_conv = e[f"gc{c}"]
            head = e[f"head{c + 1}"]
            near = jnp.concatenate([(grad_conv * kept_of(c))[1:], head[:1]], axis=0)
            far = jnp.concatenate([(grad_conv * both_of(c))[2:], head[1:]], axis=0)
            grad_product = taps[0] * grad_conv + taps[1] * near + taps[2] * far
            left = e[f"proj{c}"][:, :inner].astype(f32)
            right = e[f"proj{c}"][:, 2 * inner :].astype(f32)
            grad_projected = jnp.concatenate(
                [
                    (grad_product * right).astype(bf16),
                    e[f"go{c}"],
                    (grad_product * left).astype(bf16),
                ],
                axis=1,
            )
            grad_normed = dot_right(grad_projected, in_full).astype(bf16)
            return grad_projected, grad_normed

        needs = [f"gm{c}", f"proj{c}", f"longer{c}", f"conv{c}"]
        gives = [f"gc{c}", f"go{c}", f"tap{c}", f"head{c}"]
        gives += [f"head{chunks}"] if c == 0 else []
        add(f"backA{c}", needs, gives, 5.0, (2, c))(run_a)
        needs = [f"gc{c}", f"go{c}", f"proj{c}", f"head{c + 1}"]
        add(f"backB{c}", needs, [f"gp{c}", f"gn1{c}"], 8.0, (3, c))(run_b)

        def run_gain(e):
            value = tokens_of(c).astype(f32)
            scaled = value * rms_scale(value)
            return (jnp.sum(e[f"gn1{c}"].astype(f32) * scaled, axis=0),)

        needs = [f"gn1{c}", f"gn1{chunks - 1}", f"four{(c + 1) // 2}_sum"]
        add(f"gain{c}", needs, [f"g1{c}"], 2.0, (3.5, c))(run_gain)

    def fourth(c):
        def run(e):
            value = own_half(tokens_of(c)).astype(f32)
            inverse = rms_scale(value)
            scaled = value * inverse
            grad_normed = e[f"four{c}_sum"]
            grad_tokens = e[f"gh{c}"] + norm_back(grad_normed, scaled, inverse, gain_one)
            return (grad_tokens.astype(bf16),)

        add(f"fourth{c}", [f"four{c}_sum", f"gh{c}"], [f"gtown{c}"], 3.0, (1, c))(run)
        sums.append(Sum(f"four{c}", f"gn1{c}", f"fourth{c}", f"gtown{c}", f"gt{c}", (2, c), (4, c)))

    for c in range(chunks):
        mix(c)
    for c in range(chunks):
        first(c)
        feed(c)
        second(c)
        back(c)
        fourth(c)

    third(chunks // 2)
    for c in range(chunks // 2, chunks):
        third_line(c)

    def joined(e, name):
        return jnp.concatenate([e[f"{name}{c}"] for c in range(chunks)], axis=0)

    def names(*kinds):
        return [f"{kind}{c}" for kind in kinds for c in range(chunks)]

    def scattered_sum(name, needs, run, cost, order, dim, lasts):
        add(f"{name}_part", needs, [f"{name}_part"], cost, (5, order))(run)

        def call(e):
            return (lax.psum_scatter(e[f"{name}_part"], "seq", scatter_dimension=dim, tiled=True),)

        add(f"call_{name}", [f"{name}_part"], [name], 0.0, (2.6, 9 + order), lasts)(call)

    def down_part(e):
        return (dot_left(joined(e, "act"), out_grad).astype(bf16),)

    def gate_part(e):
        return (dot_left(joined(e, "n2"), joined(e, "gg")).astype(bf16),)

    def up_part(e):
        return (dot_left(joined(e, "n2"), joined(e, "gu")).astype(bf16),)

    def mixer_part(e):
        return (mixer_products(normed_one, joined(e, "gp"), joined(e, "gm"), joined(e, "gated")),)

    scattered_sum("down_grad", names("act"), down_part, 12.0, 0, 1, 4)
    scattered_sum("gate_grad", names("n2", "gg"), gate_part, 11.0, 1, 0, 4)
    scattered_sum("up_grad", names("n2", "gu"), up_part, 11.0, 1.5, 0, 4)
    scattered_sum("mixer_grad", names("gm", "gated", "gp"), mixer_part, 18.0, 2, 0, 3)

    def total(e, kind):
        return sum(e[f"{kind}{c}"] for c in range(chunks))

    def small(e):
        owner = (place == 0) | (place == line - 1)
        gains = jnp.stack([total(e, "g1"), jnp.where(owner, total(e, "g2"), 0.0)])
        return (jnp.concatenate([gains.reshape(-1, inner), total(e, "tap")], axis=0),)

    add("small", names("g1", "g2", "tap"), ["small0"], 2.0, (4, 9))(small)
    turn = 0
    for axis in ("seq", "tp"):
        for bit in bits_of(axis):

            def run(e, axis=axis, bit=bit, turn=turn):
                value = e[f"small{turn}"]
                if axis == "seq":
                    return (value + paired(value, axis, bit),)
                gains = value[:-3] + paired(value[:-3], axis, bit)
                return (jnp.concatenate([gains, value[-3:]], axis=0),)

            add(f"small{turn + 1}", [f"small{turn}"], [f"small{turn + 1}"], 2.0, (4, 10))(run)
            turn += 1

    def rows_put(name, needs, first, step, after=()):
        def run(e):
            block = e[needs[0]].astype(f32 if name == "tokens_grad" else bf16)
            if len(needs) == 1:
                return (jnp.pad(block, ((0, count - block.shape[0]), (0, 0))),)
            return (lax.dynamic_update_slice(e[needs[1]], block, (first, 0)),)

        add(f"{name}_{step}", needs + list(after), [f"{name}{step}"], 2.0, (4.6, step))(run)

    for c in range(chunks):
        so_far = [f"tokens_grad{c - 1}"] if c else []
        rows_put("tokens_grad", [f"gt{c}"] + so_far, c * rows, c)
    rows_put("block_out", ["out0"], 0, 0, ["small0"])
    for c in range(chunks // 2, chunks):
        step = c - chunks // 2 + 1
        rows_put("block_out", [f"out{c}", f"block_out{step - 1}"], c * rows, step)

    def widened(name):
        add(f"{name}_wide", [f"{name}_grad", "small0"], [f"{name}_wide"], 2.0, (4.7, 0))(
            lambda e: (e[f"{name}_grad"].astype(f32),)
        )

    for name in ("down", "gate", "up"):
        widened(name)

    def mixer_wide(e):
        mixer_grad = e["mixer_grad"].astype(f32)
        return mixer_grad[:, : 3 * inner].reshape(in_weight.shape), mixer_grad[:, 3 * inner :].T

    add("mixer_wide", ["mixer_grad"], ["in_wide", "out_wide"], 3.0, (4.5, 1))(mixer_wide)

    slots = plan(steps, sums, line, 16.0)
    run_slots(slots, sums, env, line, place, half)

    gains = env[f"small{turn}"][:-3].reshape(2, width)
    return (
        env[f"block_out{chunks - chunks // 2}"],
        env[f"tokens_grad{chunks - 1}"],
        env["in_wide"],
        env[f"small{turn}"][-3:],
        env["out_wide"],
        env["gate_wide"],
        env["up_wide"],
        env["down_wide"],
        gains[0],
        gains[1],
    )


def run_slots(slots, sums, env, line, place, half):
    up, down = {}, {}
    last = line - 1
    fresh, later = [], {}
    awaited = f"head{chunks}"

    def chosen(options):
        value = None
        for position, option in sorted(options.items(), reverse=True):
            if value is None or option is value:
                value = option
            else:
                value = jnp.where(place == position, option, value)
        return value

    def local_parts(slot):
        up_options, down_options = {}, {}
        for one in sums:
            hop = slot - one.start
            if 0 <= hop < last:
                part = env[one.part]
                up_options[hop] = part[:half]
                down_options[last - hop] = part[half:]
            hop = slot - one.back
            if 0 <= hop < last:
                value = env[one.own] if hop == 0 else None
                up_options[hop] = down_options[last - hop] = value
        return up_options, down_options

    def mixed(options):
        if all(value is None for value in options.values()):
            return None
        return chosen({p: 0.0 if value is None else value for p, value in options.items()})

    ready = None
    for slot, steps in enumerate(slots):
        up_options, down_options = local_parts(slot)
        sending = len(up_options) > 0
        if sending:
            send_up, send_down = ready if ready is not None else (None, None)
            if ready is None:
                send_up, send_down = mixed(up_options), mixed(down_options)
            if slot - 1 in up:
                send_up = up[slot - 1] if send_up is None else send_up + up[slot - 1]
                send_down = down[slot - 1] if send_down is None else send_down + down[slot - 1]
        for one in sums:
            if slot == one.back + last:
                own, begin = env[one.own], one.back
                top = {last: own} | {last - 1 - j: down[begin + j] for j in range(last)}
                bottom = {0: own} | {1 + j: up[begin + j] for j in range(last)}
                block = jnp.concatenate([chosen(top), chosen(bottom)], axis=0)
                env[one.joined] = block
        keys = list(fresh) + later.get(slot, [])
        for step in steps:
            keys += [name for name in step.needs if name in env and name not in keys]
        tied = [env[name] for name in keys]
        if sending:
            send_up, send_down, tied = lax.optimization_barrier((send_up, send_down, tied))
            up[slot] = lax.ppermute(send_up, "tp", [(p, p + 1) for p in up_options])
            down[slot] = lax.ppermute(send_down, "tp", [(p, p - 1) for p in down_options])
        elif tied:
            tied = lax.optimization_barrier(tied)
        env.update(zip(keys, tied))
        for one in sums:
            if slot == one.start + last:
                part = env[one.part]
                above = part[:half].astype(f32) + up[slot - 1].astype(f32)
                below = part[half:].astype(f32) + down[slot - 1].astype(f32)
                env[one.name + "_sum"] = jnp.where(place == last, above, below)
        fresh = []
        for step in steps:
            env.update(zip(step.gives, step.run(env)))
            if step.lasts:
                later.setdefault(step.until, []).extend(step.gives)
            else:
                fresh += [name for name in step.gives if name != awaited]
        ready = lax.optimization_barrier(tuple(mixed(o) for o in local_parts(slot + 1)))


def solution(mesh):
    in_specs = (
        P("seq", None),
        P("seq"),
        P(),
        P("seq", None, "tp"),
        P(None, "tp"),
        P("tp", "seq"),
        P(),
        P("seq", "tp"),
        P("seq", "tp"),
        P("tp", "seq"),
        P("seq", None),
    )
    out_specs = (
        P("seq", None),
        P("seq", None),
        P("seq", None, "tp"),
        P(None, "tp"),
        P("tp", "seq"),
        P("seq", "tp"),
        P("seq", "tp"),
        P("tp", "seq"),
        P(),
        P(),
    )
    return jax.shard_map(local, mesh=mesh, in_specs=in_specs, out_specs=out_specs, check_vma=False)
```
